128 devices in a mesh: seq: 16 (over z, x), dp: 8 (over y, core).
Axes of the slice: x: 4, y: 4, z: 4, core: 2. Of those that a mesh axis runs over, the one named last changes fastest.
Arguments:
- saved_query: bfloat16 [8, 2048, 2048], P('dp', 'seq'), may hold values from -21 to 21
- saved_key: bfloat16 [8, 2048, 2048], P('dp', 'seq'), may hold values from -4 to 4
- saved_value: bfloat16 [8, 2048, 2048], P('dp', 'seq'), may hold values from -6 to 6
- out_grad: bfloat16 [8, 2048, 2048], P('dp', 'seq'), may hold values from -6 to 6
- out_weight: bfloat16 [2048, 2048], replicated, may hold values from -0.125 to 0.125
- block_index: int32 [8, 16, 8], P('dp'), may hold values from 0 to 15, as said below
- block_count: int32 [8, 16], P('dp'), may hold values from 1 to 8, as said below
Outputs:
- query_grad: bfloat16 [8, 2048, 2048], P('dp', 'seq')
- key_grad: bfloat16 [8, 2048, 2048], P('dp', 'seq')
- value_grad: bfloat16 [8, 2048, 2048], P('dp', 'seq')
- out_weight_grad: float32 [2048, 2048], P('seq')
The draws below stay inside these ranges and needn't reach their ends.
Inputs may be any that keep to these rules, and one draw needn't show every extreme that they name: `block_index`: slot 0 of query block i names block i itself; the live slots of a query block name distinct key blocks; slots past block_count name key blocks too and are ignored. `block_count`: in each replica some query block has 8 live slots and some other has one.
All inputs are finite; a program needn't handle non-finite values.
Results may differ from the reference program's by a relative error of at most 0.023.
Values may be sent and summed in bfloat16 or wider, within the bound.
No kernel may reach another device: no remote copies, remote signals or barrier semaphores. Data moves between devices by JAX's collectives and lax.ppermute only.
A program may use at most 128 MiB of HBM per device.

```python
import jax
import jax.numpy as jnp
from jax import lax

D = 2048
HEADS = 16
HD = 128
BLK = 128
KMAX = 8
HW = 2048
SEQ = 2048
NQB = 16
REPLICAS = 8
ALL_TOKENS = 16384


def draw_saved_key(key, part):
    key = jax.random.fold_in(key, 21)
    return jax.random.truncated_normal(key, -4.0, 4.0, (REPLICAS, SEQ, HW), jnp.float32).astype(jnp.bfloat16)


def draw_saved_query(key, part):
    key = jax.random.fold_in(key, 22)
    fresh_key = jax.random.fold_in(key, 0)
    return jax.random.truncated_normal(fresh_key, -4.0, 4.0, (REPLICAS, SEQ, HW), jnp.float32).astype(jnp.bfloat16)


def draw_block_index(key, part):
    key = jax.random.fold_in(key, 11)
    row_keys = jax.random.split(key, REPLICAS * NQB)
    shuffled = jax.vmap(lambda single: jax.random.permutation(single, NQB - 1))(row_keys)[:, :KMAX - 1]
    own_block = jnp.arange(REPLICAS * NQB, dtype=jnp.int32) % NQB
    others = (own_block[:, None] + 1 + shuffled.astype(jnp.int32)) % NQB
    joined = jnp.concatenate([own_block[:, None], others], axis=1)
    return joined.reshape(REPLICAS, NQB, KMAX).astype(jnp.int32)


def draw_block_count(key, part):
    key = jax.random.fold_in(key, 12)
    count_key, high_key, offset_key = jax.random.split(key, 3)
    counts = jax.random.randint(count_key, (REPLICAS, NQB), 1, KMAX + 1, jnp.int32)
    high_row = jax.random.randint(high_key, (REPLICAS, 1), 0, NQB, jnp.int32)
    offset = jax.random.randint(offset_key, (REPLICAS, 1), 1, NQB, jnp.int32)
    low_row = (high_row + offset) % NQB
    position = jnp.arange(NQB, dtype=jnp.int32)[None, :]
    counts = jnp.where(position == high_row, KMAX, jnp.where(position == low_row, 1, counts))
    return counts.astype(jnp.int32)


def block_levels(key, dims, shards, least, largest):
    loudness, own = 1.0, jax.random.fold_in(key, 6)
    for axis_at, parts in shards:
        steps = jnp.exp(jax.random.uniform(jax.random.fold_in(own, axis_at), (parts,), jnp.float32, least / len(shards), largest / len(shards)))
        loudness = loudness * jnp.repeat(steps, dims[axis_at] // parts).reshape([-1 if axis == axis_at else 1 for axis in range(len(dims))])
    return loudness


def centred(stream_key, dims, width, reach, shards=(), kind=jnp.bfloat16):
    values = width * jax.random.normal(stream_key, dims, jnp.float32)
    if shards:
        values = values * block_levels(stream_key, dims, shards, -0.22, 0.18)
    return jnp.clip(values, -reach, reach).astype(kind)


def setup_inputs(seed: int = 0) -> dict:
    seeds = jax.random.split(jax.random.key(seed), 8)
    return {
        "saved_query": draw_saved_query(jax.random.fold_in(seeds[7], 71), 0),
        "saved_key": draw_saved_key(jax.random.fold_in(seeds[7], 71), 0),
        "saved_value": centred(seeds[2], (REPLICAS, SEQ, HW), 1.0, 6.0, ((0, 8), (1, 16))),
        "out_grad": centred(seeds[3], (REPLICAS, SEQ, D), 1.0, 6.0, ((0, 8), (1, 16))),
        "out_weight": centred(seeds[4], (HW, D), HW ** -0.5, 0.125),
        "block_index": draw_block_index(jax.random.fold_in(seeds[7], 71), 0),
        "block_count": draw_block_count(jax.random.fold_in(seeds[7], 71), 0),
    }


NEG_FILL = -1e30


def head_backward(head_inputs, block_ids, live_count):
    query_rows, key_rows, value_rows, cot_rows = head_inputs
    head_size = query_rows.shape[-1]
    score_scale = head_size ** -0.5
    query_blocks = query_rows.reshape(-1, BLK, head_size).astype(jnp.float32)
    cot_blocks = cot_rows.reshape(-1, BLK, head_size).astype(jnp.float32)
    key_blocks = key_rows.reshape(-1, BLK, head_size)
    value_blocks = value_rows.reshape(-1, BLK, head_size)
    key_chosen = key_blocks[block_ids].astype(jnp.float32)
    value_chosen = value_blocks[block_ids].astype(jnp.float32)
    live_slots = jnp.arange(KMAX)[None, :] < live_count[:, None]
    scores = jnp.einsum("bid,bkjd->bikj", query_blocks, key_chosen) * score_scale
    scores = jnp.where(live_slots[:, None, :, None], scores, NEG_FILL)
    row_peak = jnp.max(scores, axis=(2, 3), keepdims=True)
    weights = jnp.exp(scores - row_peak)
    attn_probs = weights / jnp.sum(weights, axis=(2, 3), keepdims=True)
    probs_low = attn_probs.astype(jnp.bfloat16)
    attention_wide = jnp.einsum("bikj,bkjd->bid", probs_low.astype(jnp.float32), value_chosen)
    row_delta = jnp.sum(cot_blocks * attention_wide, axis=-1)
    cot_scores = jnp.einsum("bid,bkjd->bikj", cot_blocks, value_chosen)
    score_cot = (attn_probs * (cot_scores - row_delta[:, :, None, None]) * score_scale).astype(jnp.bfloat16)
    query_grad = jnp.einsum("bikj,bkjd->bid", score_cot.astype(jnp.float32), key_chosen)
    key_parts = jnp.einsum("bikj,bid->bkjd", score_cot.astype(jnp.float32), query_blocks)
    value_parts = jnp.einsum("bikj,bid->bkjd", probs_low.astype(jnp.float32), cot_blocks)
    zero_grid = jnp.zeros(key_blocks.shape, jnp.float32)
    key_grad = zero_grid.at[block_ids].add(key_parts)
    value_grad = zero_grid.at[block_ids].add(value_parts)
    row_shape = query_rows.shape
    return (attention_wide.astype(jnp.bfloat16).reshape(row_shape),
            query_grad.astype(jnp.bfloat16).reshape(row_shape),
            key_grad.astype(jnp.bfloat16).reshape(row_shape),
            value_grad.astype(jnp.bfloat16).reshape(row_shape))


def by_heads(rows):
    return rows.reshape(SEQ, HEADS, HD).transpose(1, 0, 2)


def from_heads(rows):
    return rows.transpose(1, 0, 2).reshape(SEQ, HEADS * HD)


def replica_backward(inputs):
    query_rows, key_rows, value_rows, cot_rows, block_ids, live_count = inputs

    def one_head(head_inputs):
        return head_backward(head_inputs, block_ids, live_count)

    results = lax.map(one_head, (by_heads(query_rows), by_heads(key_rows), by_heads(value_rows), by_heads(cot_rows)))
    return (from_heads(results[0]), from_heads(results[1]), from_heads(results[2]), from_heads(results[3]))


def reference(saved_query, saved_key, saved_value, out_grad, out_weight, block_index, block_count):
    out_cot = jnp.einsum("rte,he->rth", out_grad.astype(jnp.float32), out_weight.astype(jnp.float32)).astype(jnp.bfloat16)
    attention, query_grad, key_grad, value_grad = lax.map(
        replica_backward, (saved_query, saved_key, saved_value, out_cot, block_index, block_count))
    weight_sum = jnp.einsum("rth,rte->he", attention.astype(jnp.float32), out_grad.astype(jnp.float32))
    out_weight_grad = weight_sum * (ALL_TOKENS ** -0.5)
    return query_grad, key_grad, value_grad, out_weight_grad
```

```python
import functools

import jax
import jax.numpy as jnp
from jax import lax
from jax.experimental import pallas as pl
from jax.experimental.pallas import tpu as pltpu
from jax.sharding import PartitionSpec as P

HD = 128
BLK = 128
LOG2E = 1.4426950408889634
VMEM = pl.BlockSpec(memory_space=pltpu.VMEM)
SMEM = pl.BlockSpec(memory_space=pltpu.SMEM)
NN = (((1,), (0,)), ((), ()))
NT = (((1,), (1,)), ((), ()))


def dot(a, b, dims=NN):
    return lax.dot_general(a, b, dims, preferred_element_type=jnp.float32)


def pack_kernel(q_ref, k_ref, v_ref, g_ref, w_ref, out_ref):
    cot = dot(g_ref[...], w_ref[...], NT).astype(jnp.bfloat16)
    for h in range(out_ref.shape[0]):
        cols = slice(h * HD, (h + 1) * HD)
        out_ref[h, :, 0:HD] = q_ref[:, cols]
        out_ref[h, :, HD : 2 * HD] = k_ref[:, cols]
        out_ref[h, :, 2 * HD : 3 * HD] = v_ref[:, cols]
        out_ref[h, :, 3 * HD : 4 * HD] = cot[:, cols]


def pack(q, k, v, g, w, steps=8):
    tokens, width = q.shape
    heads = width // HD
    part = pl.BlockSpec((tokens, width // steps), lambda i: (0, i))
    return pl.pallas_call(
        pack_kernel,
        grid=(steps,),
        in_specs=[
            part,
            part,
            part,
            pl.BlockSpec((tokens, g.shape[1]), lambda i: (0, 0)),
            pl.BlockSpec((width // steps, w.shape[1]), lambda i: (i, 0)),
        ],
        out_specs=pl.BlockSpec((heads // steps, tokens, 4 * HD), lambda i: (i, 0, 0)),
        out_shape=jax.ShapeDtypeStruct((heads, tokens, 4 * HD), jnp.bfloat16),
        compiler_params=pltpu.CompilerParams(vmem_limit_bytes=32 * 2**20),
        cost_estimate=pl.CostEstimate(
            flops=2 * tokens * width * width, bytes_accessed=12 * 2**20, transcendentals=0
        ),
        name="pack",
    )(q, k, v, g, w)


def attention_kernel(ids_ref, count_ref, in_ref, att_ref, grad_ref, kvt_ref, acc_ref):
    blocks = in_ref.shape[0]
    slots = ids_ref.shape[1]
    scale = HD**-0.5

    for j in range(blocks):
        kvt_ref[j] = in_ref[j, :, HD : 3 * HD].T
    acc_ref[...] = jnp.zeros_like(acc_ref)

    def block_step(i, carry):
        q = in_ref[i, :, 0:HD]
        c = in_ref[i, :, 3 * HD : 4 * HD]
        zero = jnp.zeros((HD, BLK), jnp.bfloat16)
        left = jnp.concatenate(
            [
                jnp.concatenate([q.T, zero], axis=1),
                jnp.concatenate([zero, c.T], axis=1),
            ],
            axis=0,
        )
        right = jnp.concatenate(
            [
                jnp.concatenate([q, zero], axis=1),
                jnp.concatenate([zero, c], axis=1),
            ],
            axis=0,
        )

        def live(n):
            js = [ids_ref[i, s] for s in range(n)]
            kv = jnp.concatenate([in_ref[j, :, HD : 3 * HD] for j in js], axis=0)
            both = dot(kv, left)
            s = both[:, :BLK]
            dp = both[:, BLK:]
            peak = jnp.max(s, axis=0, keepdims=True)
            w = jnp.exp2((s - peak) * (scale * LOG2E))
            p = w * (1.0 / jnp.sum(w, axis=0, keepdims=True))
            low = p.astype(jnp.bfloat16)
            delta = jnp.sum(low.astype(jnp.float32) * dp, axis=0, keepdims=True)
            ds = (p * (dp - delta) * scale).astype(jnp.bfloat16)
            pair = jnp.concatenate([ds, low], axis=1)
            grads = dot(pair, right)
            for s, j in enumerate(js):
                acc_ref[j] += grads[s * BLK : (s + 1) * BLK]
            kvt = jnp.concatenate([kvt_ref[j] for j in js], axis=1)
            out = dot(kvt, pair)
            grad_ref[i, :, 0:HD] = out[:HD, :BLK].T.astype(jnp.bfloat16)
            att_ref[i] = out[HD:, BLK:].astype(jnp.bfloat16)

        for n in range(1, slots + 1):
            pl.when(count_ref[i] == n)(functools.partial(live, n))
        return carry

    lax.fori_loop(0, blocks, block_step, 0)
    for j in range(blocks):
        grad_ref[j, :, HD : 3 * HD] = acc_ref[j].astype(jnp.bfloat16)


def attention_backward(ids, count, rows):
    blocks = rows.shape[0]
    return pl.pallas_call(
        attention_kernel,
        in_specs=[SMEM, SMEM, VMEM],
        out_specs=[VMEM, VMEM],
        out_shape=[
            jax.ShapeDtypeStruct((blocks, HD, BLK), jnp.bfloat16),
            jax.ShapeDtypeStruct((blocks, BLK, 3 * HD), jnp.bfloat16),
        ],
        scratch_shapes=[
            pltpu.VMEM((blocks, 2 * HD, BLK), jnp.bfloat16),
            pltpu.VMEM((blocks, BLK, 2 * HD), jnp.float32),
        ],
        compiler_params=pltpu.CompilerParams(vmem_limit_bytes=48 * 2**20),
        cost_estimate=pl.CostEstimate(
            flops=2 * 5 * 128 * 128**3, bytes_accessed=4 * 2**20, transcendentals=2**21
        ),
        name="attention_backward",
    )(ids, count, rows)


def unpack_kernel(in_ref, q_ref, k_ref, v_ref):
    for h in range(in_ref.shape[0]):
        cols = slice(h * HD, (h + 1) * HD)
        q_ref[:, cols] = in_ref[h, :, 0:HD]
        k_ref[:, cols] = in_ref[h, :, HD : 2 * HD]
        v_ref[:, cols] = in_ref[h, :, 2 * HD : 3 * HD]


def unpack(rows, steps=4):
    heads, tokens, _ = rows.shape
    shape = jax.ShapeDtypeStruct((tokens, heads * HD), jnp.bfloat16)
    part = pl.BlockSpec((tokens, heads * HD // steps), lambda i: (0, i))
    return pl.pallas_call(
        unpack_kernel,
        grid=(steps,),
        in_specs=[pl.BlockSpec((heads // steps, tokens, 3 * HD), lambda i: (i, 0, 0))],
        out_specs=[part] * 3,
        out_shape=[shape] * 3,
        cost_estimate=pl.CostEstimate(flops=0, bytes_accessed=3 * 2**20, transcendentals=0),
        name="unpack",
    )(rows)


def on_device(saved_query, saved_key, saved_value, out_grad, out_weight, block_index, block_count):
    grad_rows = out_grad[0]
    tokens = grad_rows.shape[0]
    seq_devices = lax.axis_size("seq")
    dp_devices = lax.axis_size("dp")
    grad_all = lax.all_gather(grad_rows, "seq", tiled=True)

    packed = pack(saved_query[0], saved_key[0], saved_value[0], grad_rows, out_weight)
    rows = lax.all_to_all(packed, "seq", split_axis=0, concat_axis=0, tiled=True)
    attention, grads = attention_backward(block_index[0], block_count[0], rows)
    back = lax.all_to_all(grads, "seq", split_axis=0, concat_axis=0, tiled=True)
    query_grad, key_grad, value_grad = unpack(back)

    weight_scale = (tokens * seq_devices * dp_devices) ** (-0.5)
    part = jnp.einsum(
        "bht,bte->he",
        attention,
        grad_all.reshape(seq_devices, tokens, -1),
        preferred_element_type=jnp.float32,
    ).astype(jnp.bfloat16)
    shares = lax.all_to_all(
        part.reshape(dp_devices, HD // dp_devices, -1), "dp", split_axis=0, concat_axis=0, tiled=True
    )
    share = jnp.sum(shares.astype(jnp.float32), axis=0).astype(jnp.bfloat16)
    total = lax.all_gather(share, "dp", tiled=True)
    return (
        query_grad[None],
        key_grad[None],
        value_grad[None],
        total.astype(jnp.float32) * weight_scale,
    )


def solution(mesh):
    placed = P("dp", "seq", None)
    return jax.shard_map(
        on_device,
        mesh=mesh,
        in_specs=(placed, placed, placed, placed, P(), P("dp", None, None), P("dp", None)),
        out_specs=(placed, placed, placed, P("seq", None)),
        check_vma=False,
    )
```

```python
import functools

import jax
import jax.numpy as jnp
from jax import lax
from jax.experimental import pallas as pl
from jax.experimental.pallas import tpu as pltpu
from jax.sharding import PartitionSpec as P

HD = 128
BLK = 128
SIDE = 4
LOG2E = 1.4426950408889634
SCALE = HD**-0.5
MIB = 2**20
BIG = pltpu.CompilerParams(vmem_limit_bytes=60 * MIB)
VMEM = pl.BlockSpec(memory_space=pltpu.VMEM)
SMEM = pl.BlockSpec(memory_space=pltpu.SMEM)
NN = (((1,), (0,)), ((), ()))
NT = (((1,), (1,)), ((), ()))


def dot(a, b, dims=NN):
    return lax.dot_general(a, b, dims, preferred_element_type=jnp.float32)


def cost(flops, size, exps=0):
    return pl.CostEstimate(flops=flops, bytes_accessed=size, transcendentals=exps)


def shaped(*dims, dtype=jnp.bfloat16):
    return jax.ShapeDtypeStruct(dims, dtype)


def pack_kernel(q_ref, k_ref, v_ref, out_ref):
    for h in range(out_ref.shape[0]):
        cols = slice(h * HD, (h + 1) * HD)
        out_ref[h, :, 0:HD] = q_ref[:, cols]
        out_ref[h, :, HD : 2 * HD] = k_ref[:, cols]
        out_ref[h, :, 2 * HD : 3 * HD] = v_ref[:, cols]


def pack(q, k, v, steps=4):
    tokens, width = q.shape
    heads = width // HD
    part = pl.BlockSpec((tokens, width // steps), lambda i: (0, i))
    return pl.pallas_call(
        pack_kernel,
        grid=(steps,),
        in_specs=[part] * 3,
        out_specs=pl.BlockSpec((heads // steps, tokens, 3 * HD), lambda i: (i, 0, 0)),
        out_shape=shaped(heads, tokens, 3 * HD),
        compiler_params=BIG,
        cost_estimate=cost(0, 3 * MIB),
        name="pack",
    )(q, k, v)


def cot_kernel(g_ref, w_ref, out_ref, copy_ref):
    cot = dot(g_ref[...], w_ref[...], NT).astype(jnp.bfloat16)
    for h in range(out_ref.shape[0]):
        out_ref[h] = cot[:, h * HD : (h + 1) * HD]

    @pl.when(pl.program_id(0) == 0)
    def _():
        copy_ref[...] = g_ref[...]


def out_cotangent(g, w, steps=8):
    tokens, width = g.shape
    rows = w.shape[0]
    heads = rows // HD
    whole = pl.BlockSpec((tokens, width), lambda i: (0, 0))
    return pl.pallas_call(
        cot_kernel,
        grid=(steps,),
        in_specs=[whole, pl.BlockSpec((rows // steps, width), lambda i: (i, 0))],
        out_specs=[pl.BlockSpec((heads // steps, tokens, HD), lambda i: (i, 0, 0)), whole],
        out_shape=[shaped(heads, tokens, HD), shaped(tokens, width)],
        compiler_params=BIG,
        cost_estimate=cost(2 * tokens * rows * width, 9 * MIB),
        name="out_cotangent",
    )(g, w)


def forward_kernel(ids_ref, count_ref, in_ref, att_ref, lse_ref, vt_ref):
    blocks = in_ref.shape[0]
    for j in range(blocks):
        vt_ref[j] = in_ref[j, :, 2 * HD : 3 * HD].T

    def block_step(i, carry):
        qt = in_ref[i, :, 0:HD].T

        def live(n):
            js = [ids_ref[i, s] for s in range(n)]
            s = dot(jnp.concatenate([in_ref[j, :, HD : 2 * HD] for j in js], axis=0), qt)
            peak = jnp.max(s, axis=0, keepdims=True)
            w = jnp.exp2((s - peak) * (SCALE * LOG2E))
            total = jnp.sum(w, axis=0, keepdims=True)
            low = (w * (1.0 / total)).astype(jnp.bfloat16)
            att = dot(jnp.concatenate([vt_ref[j] for j in js], axis=1), low)
            att_ref[i] = att.astype(jnp.bfloat16)
            lse_ref[i, 0:1, :] = peak
            lse_ref[i, 1:2, :] = 1.0 / total

        for n in range(1, ids_ref.shape[1] + 1):
            pl.when(count_ref[i] == n)(functools.partial(live, n))
        return carry

    lax.fori_loop(0, blocks, block_step, 0)


def attention_forward(ids, count, rows):
    blocks = rows.shape[0]
    return pl.pallas_call(
        forward_kernel,
        in_specs=[SMEM, SMEM, VMEM],
        out_specs=[VMEM, VMEM],
        out_shape=[shaped(blocks, HD, BLK), shaped(blocks, 8, BLK, dtype=jnp.float32)],
        scratch_shapes=[pltpu.VMEM((blocks, HD, BLK), jnp.bfloat16)],
        compiler_params=BIG,
        cost_estimate=cost(2 * 2 * 128 * 128**3, 2 * MIB, 2**21),
        name="attention_forward",
    )(ids, count, rows)


def backward_kernel(ids_ref, count_ref, in_ref, cot_ref, lse_ref, grad_ref, kt_ref, acc_ref):
    blocks = in_ref.shape[0]
    for j in range(blocks):
        kt_ref[j] = in_ref[j, :, HD : 2 * HD].T
    acc_ref[...] = jnp.zeros_like(acc_ref)

    def block_step(i, carry):
        q = in_ref[i, :, 0:HD]
        c = cot_ref[i]
        zero = jnp.zeros((HD, BLK), jnp.bfloat16)
        left = jnp.concatenate(
            [
                jnp.concatenate([q.T, zero], axis=1),
                jnp.concatenate([zero, c.T], axis=1),
            ],
            axis=0,
        )
        right = jnp.concatenate(
            [
                jnp.concatenate([q, zero], axis=1),
                jnp.concatenate([zero, c], axis=1),
            ],
            axis=0,
        )
        peak = lse_ref[i, 0:1, :]
        inverse = lse_ref[i, 1:2, :]

        def live(n):
            js = [ids_ref[i, s] for s in range(n)]
            both = dot(jnp.concatenate([in_ref[j, :, HD : 3 * HD] for j in js], axis=0), left)
            dp = both[:, BLK:]
            p = jnp.exp2((both[:, :BLK] - peak) * (SCALE * LOG2E)) * inverse
            low = p.astype(jnp.bfloat16)
            delta = jnp.sum(low.astype(jnp.float32) * dp, axis=0, keepdims=True)
            ds = (p * (dp - delta) * SCALE).astype(jnp.bfloat16)
            grads = dot(jnp.concatenate([ds, low], axis=1), right)
            for s, j in enumerate(js):
                acc_ref[j] += grads[s * BLK : (s + 1) * BLK]
            dq = dot(jnp.concatenate([kt_ref[j] for j in js], axis=1), ds)
            grad_ref[i, :, 0:HD] = dq.T.astype(jnp.bfloat16)

        for n in range(1, ids_ref.shape[1] + 1):
            pl.when(count_ref[i] == n)(functools.partial(live, n))
        return carry

    lax.fori_loop(0, blocks, block_step, 0)
    for j in range(blocks):
        grad_ref[j, :, HD : 3 * HD] = acc_ref[j].astype(jnp.bfloat16)


def attention_backward(ids, count, rows, cot, lse):
    blocks = rows.shape[0]
    return pl.pallas_call(
        backward_kernel,
        in_specs=[SMEM, SMEM, VMEM, VMEM, VMEM],
        out_specs=VMEM,
        out_shape=shaped(blocks, BLK, 3 * HD),
        scratch_shapes=[
            pltpu.VMEM((blocks, HD, BLK), jnp.bfloat16),
            pltpu.VMEM((blocks, BLK, 2 * HD), jnp.float32),
        ],
        compiler_params=BIG,
        cost_estimate=cost(2 * 5 * 128 * 128**3, 4 * MIB, 2**21),
        name="attention_backward",
    )(ids, count, rows, cot, lse)


def unpack_kernel(in_ref, q_ref, k_ref, v_ref):
    for h in range(in_ref.shape[0]):
        cols = slice(h * HD, (h + 1) * HD)
        q_ref[:, cols] = in_ref[h, :, 0:HD]
        k_ref[:, cols] = in_ref[h, :, HD : 2 * HD]
        v_ref[:, cols] = in_ref[h, :, 2 * HD : 3 * HD]


def unpack(rows, steps=4):
    heads, tokens, _ = rows.shape
    part = pl.BlockSpec((tokens, heads * HD // steps), lambda i: (0, i))
    return pl.pallas_call(
        unpack_kernel,
        grid=(steps,),
        in_specs=[pl.BlockSpec((heads // steps, tokens, 3 * HD), lambda i: (i, 0, 0))],
        out_specs=[part] * 3,
        out_shape=[shaped(tokens, heads * HD)] * 3,
        compiler_params=BIG,
        cost_estimate=cost(0, 3 * MIB),
        name="unpack",
    )(rows)


def weight_kernel(place_ref, a0, a1, a2, a3, g0, g1, g2, g3, keep_ref, give_ref, lhs_ref):
    half = HD // 2

    @pl.when(pl.program_id(0) == 0)
    def _():
        x = place_ref[0]
        core = place_ref[1]
        for d, a in enumerate((a0, a1, a2, a3)):
            for t, back in enumerate((0, 1, 3, 2)):
                block = lax.rem(x + SIDE - back, SIDE)
                for side in range(2):
                    rows = a[block, pl.ds(lax.rem(core + side, 2) * half, half), :]
                    lhs_ref[side, d * half : (d + 1) * half, t * BLK : (t + 1) * BLK] = rows

    rhs = jnp.concatenate([g0[...], g1[...], g2[...], g3[...]], axis=0)
    for side, out in enumerate((keep_ref, give_ref)):
        res = dot(lhs_ref[side], rhs).astype(jnp.bfloat16)
        for d in range(SIDE):
            out[d] = res[d * half : (d + 1) * half]


def weight_part(place, atts, gs, steps=4):
    tokens, width = gs[0].shape
    half = HD // 2
    cols = width // steps
    piece = pl.BlockSpec((SIDE, HD, BLK), lambda i: (0, 0, 0))
    rows = pl.BlockSpec((tokens, cols), lambda i: (0, i))
    out = pl.BlockSpec((SIDE, half, cols), lambda i: (0, 0, i))
    return pl.pallas_call(
        weight_kernel,
        grid=(steps,),
        in_specs=[SMEM] + [piece] * 4 + [rows] * 4,
        out_specs=[out, out],
        out_shape=[shaped(SIDE, half, width)] * 2,
        scratch_shapes=[pltpu.VMEM((2, SIDE * half, SIDE * BLK), jnp.bfloat16)],
        compiler_params=BIG,
        cost_estimate=cost(2 * 512 * 512 * 2048, 5 * MIB),
        name="weight_part",
    )(place, *atts, *gs)


def shift_x(a, d):
    return lax.ppermute(a, "seq", [(s, s // SIDE * SIDE + (s + d) % SIDE) for s in range(SIDE**2)])


def shift_z(a, d):
    return lax.ppermute(a, "seq", [(s, (s + d * SIDE) % SIDE**2) for s in range(SIDE**2)])


def shift_y(a, d):
    return lax.ppermute(a, "dp", [(s, (s + 2 * d) % 8) for s in range(8)])


def sibling(a):
    return lax.ppermute(a, "dp", [(s, s ^ 1) for s in range(8)])


def wide(a):
    return a.astype(jnp.float32)


def on_device(saved_query, saved_key, saved_value, out_grad, out_weight, block_index, block_count):
    seq_at = lax.axis_index("seq")
    core = lax.axis_index("dp") % 2
    z, x = seq_at // SIDE, seq_at % SIDE
    ids, count = block_index[0], block_count[0]

    def by_seq(a):
        return lax.all_to_all(a, "seq", split_axis=0, concat_axis=0, tiled=True)

    rows = by_seq(pack(saved_query[0], saved_key[0], saved_value[0]))
    cot, grad_rows = out_cotangent(out_grad[0], out_weight)
    cot_rows = by_seq(cot)
    behind = shift_x(grad_rows, 1)
    ahead = shift_x(grad_rows, -1)
    middle = grad_rows.shape[0] // 2
    far = jnp.concatenate([shift_x(behind[:middle], 1), shift_x(ahead[middle:], -1)], axis=0)

    attention, lse = attention_forward(ids, count, rows)

    def chunk(d):
        return lax.dynamic_slice_in_dim(attention, (z + d) % SIDE * SIDE, SIDE, axis=0)

    atts = [chunk(0)] + [shift_z(chunk(d), d) for d in (1, 3, 2)]
    grads = attention_backward(ids, count, rows, cot_rows, lse)
    query_grad, key_grad, value_grad = unpack(by_seq(grads))

    place = jnp.stack([x, core]).astype(jnp.int32)
    keep, give = weight_part(place, atts, [grad_rows, behind, ahead, far])
    pair = (wide(keep) + wide(sibling(give))).astype(jnp.bfloat16)
    near = [pair[0]] + [shift_z(pair[n + 1], -d) for n, d in enumerate((1, 3, 2))]
    row = (wide(near[0]) + wide(near[1]) + wide(near[2]) + wide(near[3])).astype(jnp.bfloat16)
    above, below, across = shift_y(row, 1), shift_y(row, -1), shift_y(row, 2)
    total = ((wide(row) + wide(across)) + (wide(above) + wide(below))).astype(jnp.bfloat16)
    other = sibling(total)
    weight_scale = (BLK * SIDE**2 * 8) ** (-0.5)
    first = jnp.where(core == 0, total, other)
    second = jnp.where(core == 0, other, total)
    weight_grad = wide(jnp.concatenate([first, second], axis=0)) * weight_scale
    return query_grad[None], key_grad[None], value_grad[None], weight_grad


def solution(mesh):
    placed = P("dp", "seq", None)
    return jax.shard_map(
        on_device,
        mesh=mesh,
        in_specs=(placed, placed, placed, placed, P(), P("dp", None, None), P("dp", None)),
        out_specs=(placed, placed, placed, P("seq", None)),
        check_vma=False,
    )
```

```python
import functools

import jax
import jax.numpy as jnp
from jax import lax
from jax.experimental import pallas as pl
from jax.experimental.pallas import tpu as pltpu
from jax.sharding import PartitionSpec as P

HD = 128
BLK = 128
SIDE = 4
GROUP = 4
BACK = (0, 1, 3, 2)
NEG_FILL = -1e30
LOG2E = 1.4426950408889634
SCALE = HD**-0.5
MIB = 2**20
BIG = pltpu.CompilerParams(vmem_limit_bytes=60 * MIB)
VMEM = pl.BlockSpec(memory_space=pltpu.VMEM)
SMEM = pl.BlockSpec(memory_space=pltpu.SMEM)
NN = (((1,), (0,)), ((), ()))
NT = (((1,), (1,)), ((), ()))


def dot(a, b, dims=NN):
    return lax.dot_general(a, b, dims, preferred_element_type=jnp.float32)


def cost(flops, size, exps=0):
    return pl.CostEstimate(flops=flops, bytes_accessed=size, transcendentals=exps)


def shaped(*dims, dtype=jnp.bfloat16):
    return jax.ShapeDtypeStruct(dims, dtype)


def pack_kernel(q_ref, k_ref, v_ref, out_ref):
    for h in range(out_ref.shape[0]):
        cols = slice(h * HD, (h + 1) * HD)
        out_ref[h, :, 0:HD] = q_ref[:, cols]
        out_ref[h, :, HD : 2 * HD] = k_ref[:, cols]
        out_ref[h, :, 2 * HD : 3 * HD] = v_ref[:, cols]


def pack(q, k, v, steps=4):
    tokens, width = q.shape
    heads = width // HD
    part = pl.BlockSpec((tokens, width // steps), lambda i: (0, i))
    return pl.pallas_call(
        pack_kernel,
        grid=(steps,),
        in_specs=[part] * 3,
        out_specs=pl.BlockSpec((heads // steps, tokens, 3 * HD), lambda i: (i, 0, 0)),
        out_shape=shaped(heads, tokens, 3 * HD),
        compiler_params=BIG,
        cost_estimate=cost(0, 3 * MIB),
        name="pack",
    )(q, k, v)


def cot_kernel(g_ref, w_ref, out_ref, copy_ref):
    cot = dot(g_ref[...], w_ref[...], NT).astype(jnp.bfloat16)
    for h in range(out_ref.shape[0]):
        out_ref[h] = cot[:, h * HD : (h + 1) * HD]

    @pl.when(pl.program_id(0) == 0)
    def _():
        copy_ref[...] = g_ref[...]


def out_cotangent(g, w, steps=8):
    tokens, width = g.shape
    rows = w.shape[0]
    heads = rows // HD
    whole = pl.BlockSpec((tokens, width), lambda i: (0, 0))
    return pl.pallas_call(
        cot_kernel,
        grid=(steps,),
        in_specs=[whole, pl.BlockSpec((rows // steps, width), lambda i: (i, 0))],
        out_specs=[pl.BlockSpec((heads // steps, tokens, HD), lambda i: (i, 0, 0)), whole],
        out_shape=[shaped(heads, tokens, HD), shaped(tokens, width)],
        compiler_params=BIG,
        cost_estimate=cost(2 * tokens * rows * width, 9 * MIB),
        name="out_cotangent",
    )(g, w)


def rows_of(parts):
    return parts[0] if len(parts) == 1 else jnp.concatenate(parts, axis=0)


def cols_of(parts):
    return parts[0] if len(parts) == 1 else jnp.concatenate(parts, axis=1)


def attention_kernel(
    place_ref, ids_ref, count_ref, order_ref, in_ref, cot_ref,
    grad_ref, mine_ref, other_ref, kt_ref, vt_ref, att_ref, acc_ref,
):
    blocks = in_ref.shape[0]
    for j in range(blocks):
        kt_ref[j] = in_ref[j, :, HD : 2 * HD].T
        vt_ref[j] = in_ref[j, :, 2 * HD : 3 * HD].T
    acc_ref[...] = jnp.zeros_like(acc_ref)

    def step(at, carry):
        members = [order_ref[at * GROUP + g] for g in range(GROUP)]

        def live(n):
            slots = [[ids_ref[i, s] for s in range(n)] for i in members]
            qs = [in_ref[i, :, 0:HD] for i in members]
            cs = [cot_ref[i] for i in members]
            scores = [
                dot(rows_of([in_ref[j, :, HD : 2 * HD] for j in js]), q.T)
                for js, q in zip(slots, qs)
            ]
            cots = [
                dot(rows_of([in_ref[j, :, 2 * HD : 3 * HD] for j in js]), c.T)
                for js, c in zip(slots, cs)
            ]
            for g in range(1, GROUP):
                count = count_ref[members[g]]
                scores[g] = rows_of(
                    [
                        scores[g][s * BLK : (s + 1) * BLK] + jnp.where(s < count, 0.0, NEG_FILL)
                        for s in range(n)
                    ]
                )
            peaks = [jnp.max(s, axis=0, keepdims=True) for s in scores]
            weights = [jnp.exp2((s - m) * (SCALE * LOG2E)) for s, m in zip(scores, peaks)]
            probs = [w * (1.0 / jnp.sum(w, axis=0, keepdims=True)) for w in weights]
            lows = [p.astype(jnp.bfloat16) for p in probs]
            deltas = [
                jnp.sum(low.astype(jnp.float32) * c, axis=0, keepdims=True)
                for low, c in zip(lows, cots)
            ]
            terms = [
                (p * ((c - d) * SCALE)).astype(jnp.bfloat16)
                for p, c, d in zip(probs, cots, deltas)
            ]
            for js, term, low, q, c in zip(slots, terms, lows, qs, cs):
                key_part = dot(term, q)
                value_part = dot(low, c)
                for s, j in enumerate(js):
                    acc_ref[j, :, :HD] += key_part[s * BLK : (s + 1) * BLK]
                    acc_ref[j, :, HD:] += value_part[s * BLK : (s + 1) * BLK]
            for i, js, term, low in zip(members, slots, terms, lows):
                query_part = dot(cols_of([kt_ref[j] for j in js]), term)
                grad_ref[i, :, 0:HD] = query_part.astype(jnp.bfloat16).T
                att = dot(cols_of([vt_ref[j] for j in js]), low)
                att_ref[i] = att.astype(jnp.bfloat16)

        top = count_ref[members[0]]
        for n in range(1, ids_ref.shape[1] + 1):
            pl.when(top == n)(functools.partial(live, n))
        return carry

    lax.fori_loop(0, blocks // GROUP, step, 0)
    for j in range(blocks):
        grad_ref[j, :, HD : 3 * HD] = acc_ref[j].astype(jnp.bfloat16)
    half = blocks // 2
    at = place_ref[0]
    mine_ref[...] = att_ref[pl.ds(at * half, half)]
    other_ref[...] = att_ref[pl.ds((1 - at) * half, half)]


def attention_backward(place, ids, count, order, rows, cot):
    blocks = rows.shape[0]
    turned = pltpu.VMEM((blocks, HD, BLK), jnp.bfloat16)
    return pl.pallas_call(
        attention_kernel,
        in_specs=[SMEM] * 4 + [VMEM] * 2,
        out_specs=[VMEM] * 3,
        out_shape=[shaped(blocks, BLK, 3 * HD)] + [shaped(blocks // 2, HD, BLK)] * 2,
        scratch_shapes=[turned, turned, turned, pltpu.VMEM((blocks, BLK, 2 * HD), jnp.float32)],
        compiler_params=BIG,
        cost_estimate=cost(2 * 5 * 128 * 128**3, 4 * MIB, 2**21),
        name="attention_backward",
    )(place, ids, count, order, rows, cot)


def by_count(count):
    at = jnp.arange(count.shape[0], dtype=jnp.int32)
    level = count[None, :] == count[:, None]
    ahead = (count[None, :] > count[:, None]) | (level & (at[None, :] < at[:, None]))
    rank = jnp.sum(ahead.astype(jnp.int32), axis=1)
    return jnp.sum(jnp.where(rank[None, :] == at[:, None], at[None, :], 0), axis=1)


def unpack_kernel(in_ref, q_ref, k_ref, v_ref):
    for h in range(in_ref.shape[0]):
        cols = slice(h * HD, (h + 1) * HD)
        q_ref[:, cols] = in_ref[h, :, 0:HD]
        k_ref[:, cols] = in_ref[h, :, HD : 2 * HD]
        v_ref[:, cols] = in_ref[h, :, 2 * HD : 3 * HD]


def unpack(rows, steps=4):
    heads, tokens, _ = rows.shape
    part = pl.BlockSpec((tokens, heads * HD // steps), lambda i: (0, i))
    return pl.pallas_call(
        unpack_kernel,
        grid=(steps,),
        in_specs=[pl.BlockSpec((heads // steps, tokens, 3 * HD), lambda i: (i, 0, 0))],
        out_specs=[part] * 3,
        out_shape=[shaped(tokens, heads * HD)] * 3,
        compiler_params=BIG,
        cost_estimate=cost(0, 3 * MIB),
        name="unpack",
    )(rows)


def weight_kernel(place_ref, own, partner, *refs):
    pieces, (keep0, keep1, give0, give1, lhs_ref) = refs[: 2 * SIDE], refs[2 * SIDE :]
    half = HD // 2

    @pl.when(pl.program_id(0) == 0)
    def _():
        core, low, x = place_ref[1], place_ref[2], place_ref[3]
        for n in range(2 * SIDE):
            row = lax.rem(low + n // SIDE, 2)
            block = row * SIDE + lax.rem(x + SIDE - BACK[n % SIDE], SIDE)
            for head, att in enumerate((own, partner)):
                for side in range(2):
                    rows = att[block, pl.ds(lax.rem(core + side, 2) * half, half), :]
                    at = (2 * side + head) * half
                    lhs_ref[at : at + half, n * BLK : (n + 1) * BLK] = rows

    rhs = jnp.concatenate([piece[...] for piece in pieces], axis=0)
    res = dot(lhs_ref[...], rhs).astype(jnp.bfloat16)
    for n, out in enumerate((keep0, keep1, give0, give1)):
        out[...] = res[n * half : (n + 1) * half]


def weight_part(place, own, partner, pieces, steps=4):
    tokens, width = pieces[0].shape
    half = HD // 2
    cols = width // steps
    att = pl.BlockSpec(own.shape, lambda i: (0, 0, 0))
    rows = pl.BlockSpec((tokens, cols), lambda i: (0, i))
    out = pl.BlockSpec((half, cols), lambda i: (0, i))
    return pl.pallas_call(
        weight_kernel,
        grid=(steps,),
        in_specs=[SMEM, att, att] + [rows] * len(pieces),
        out_specs=[out] * 4,
        out_shape=[shaped(half, width)] * 4,
        scratch_shapes=[pltpu.VMEM((4 * half, len(pieces) * BLK), jnp.bfloat16)],
        compiler_params=BIG,
        cost_estimate=cost(2 * 256 * 1024 * 2048, 7 * MIB),
        name="weight_part",
    )(place, own, partner, *pieces)


def shift_x(a, d):
    return lax.ppermute(a, "seq", [(s, s // SIDE * SIDE + (s + d) % SIDE) for s in range(SIDE**2)])


def same_half(a):
    return lax.ppermute(a, "seq", [(s, s ^ SIDE) for s in range(SIDE**2)])


def other_half(a):
    return lax.ppermute(a, "seq", [(s, s ^ (3 * SIDE)) for s in range(SIDE**2)])


def shift_y(a, d):
    return lax.ppermute(a, "dp", [(s, (s + 2 * d) % 8) for s in range(8)])


def sibling(a):
    return lax.ppermute(a, "dp", [(s, s ^ 1) for s in range(8)])


def wide(a):
    return a.astype(jnp.float32)


def on_device(saved_query, saved_key, saved_value, out_grad, out_weight, block_index, block_count):
    seq_at = lax.axis_index("seq")
    core = lax.axis_index("dp") % 2
    z, x = seq_at // SIDE, seq_at % SIDE
    ids, count = block_index[0], block_count[0]
    place = jnp.stack([z // 2, core, z % 2, x]).astype(jnp.int32)

    def by_seq(a):
        return lax.all_to_all(a, "seq", split_axis=0, concat_axis=0, tiled=True)

    rows = by_seq(pack(saved_query[0], saved_key[0], saved_value[0]))
    cot, grad_rows = out_cotangent(out_grad[0], out_weight)
    cot_rows = by_seq(cot)
    beside = same_half(grad_rows)
    pieces = [grad_rows] + [shift_x(grad_rows, d) for d in (1, -1, 2)]
    pieces += [beside] + [shift_x(beside, d) for d in (1, -1)] + [same_half(pieces[3])]

    grads, mine, other = attention_backward(place, ids, count, by_count(count), rows, cot_rows)
    partner = other_half(other)
    query_grad, key_grad, value_grad = unpack(by_seq(grads))

    keep0, keep1, give0, give1 = weight_part(place, mine, partner, pieces)
    theirs = (wide(keep1) + wide(sibling(give1))).astype(jnp.bfloat16)
    row = (wide(keep0) + wide(sibling(give0)) + wide(other_half(theirs))).astype(jnp.bfloat16)
    above, below, across = shift_y(row, 1), shift_y(row, -1), shift_y(row, 2)
    total = ((wide(row) + wide(across)) + (wide(above) + wide(below))).astype(jnp.bfloat16)
    swapped = sibling(total)
    weight_scale = (BLK * SIDE**2 * 8) ** (-0.5)
    first = jnp.where(core == 0, total, swapped)
    second = jnp.where(core == 0, swapped, total)
    weight_grad = wide(jnp.concatenate([first, second], axis=0)) * weight_scale
    return query_grad[None], key_grad[None], value_grad[None], weight_grad


def solution(mesh):
    placed = P("dp", "seq", None)
    return jax.shard_map(
        on_device,
        mesh=mesh,
        in_specs=(placed, placed, placed, placed, P(), P("dp", None, None), P("dp", None)),
        out_specs=(placed, placed, placed, P("seq", None)),
        check_vma=False,
    )
```

```python
import functools

import jax
import jax.numpy as jnp
from jax import lax
from jax.experimental import pallas as pl
from jax.experimental.pallas import tpu as pltpu
from jax.sharding import PartitionSpec as P

HD = 128
BLK = 128
SIDE = 4
GROUP = 4
DEPS = 1
HOPS = (0, 1, 3, 2)
NEG_FILL = -1e30
LOG2E = 1.4426950408889634
SCALE = HD**-0.5
MIB = 2**20
BIG = pltpu.CompilerParams(vmem_limit_bytes=60 * MIB)
MEDIUM = pltpu.CompilerParams(vmem_limit_bytes=32 * MIB)
SMALL = pltpu.CompilerParams(vmem_limit_bytes=16 * MIB)
VMEM = pl.BlockSpec(memory_space=pltpu.VMEM)
ANY = pl.BlockSpec(memory_space=pl.ANY)
SMEM = pl.BlockSpec(memory_space=pltpu.SMEM)
NN = (((1,), (0,)), ((), ()))


def dot(a, b, dims=NN):
    return lax.dot_general(a, b, dims, preferred_element_type=jnp.float32)


def cost(flops, size, exps=0):
    return pl.CostEstimate(flops=flops, bytes_accessed=size, transcendentals=exps)


def shaped(*dims, dtype=jnp.bfloat16):
    return jax.ShapeDtypeStruct(dims, dtype)


def pack_kernel(q, k, v, g, w, out, q_in, k_in, v_in, g_in, w_in, turned, packed, sems, done):
    parts, height, _ = w_in.shape
    heads = packed.shape[0] // parts
    loads = [
        pltpu.make_async_copy(src, dst, sems.at[n])
        for n, (src, dst) in enumerate(((g, g_in), (q, q_in), (k, k_in), (v, v_in)))
    ]
    loads += [
        pltpu.make_async_copy(w.at[pl.ds(p * height, height)], w_in.at[p], sems.at[4 + p])
        for p in range(parts)
    ]
    for load in loads:
        load.start()
    loads[0].wait()
    for n in range(g_in.shape[1] // BLK):
        turned[n * BLK : (n + 1) * BLK, :] = g_in[:, n * BLK : (n + 1) * BLK].T
    for load in loads[1:4]:
        load.wait()
    for h in range(packed.shape[0]):
        cols = slice(h * HD, (h + 1) * HD)
        packed[h, :, 0:HD] = q_in[:, cols]
        packed[h, :, HD : 2 * HD] = k_in[:, cols]
        packed[h, :, 2 * HD : 3 * HD] = v_in[:, cols]
    stores = []
    for p in range(parts):
        loads[4 + p].wait()
        cot = dot(w_in[p], turned[...]).astype(jnp.bfloat16)
        for n in range(heads):
            packed[p * heads + n, :, 3 * HD : 4 * HD] = cot[n * HD : (n + 1) * HD]
        some = pl.ds(p * heads, heads)
        stores.append(pltpu.make_async_copy(packed.at[some], out.at[some], done.at[p]))
        stores[-1].start()
    for store in stores:
        store.wait()


def pack(q, k, v, g, w, parts=8):
    tokens, width = q.shape
    rows, depth = w.shape
    heads = rows // HD
    return pl.pallas_call(
        pack_kernel,
        in_specs=[ANY] * 5,
        out_specs=ANY,
        out_shape=shaped(heads, tokens, 4 * HD),
        scratch_shapes=[
            pltpu.VMEM((tokens, width), jnp.bfloat16),
            pltpu.VMEM((tokens, width), jnp.bfloat16),
            pltpu.VMEM((tokens, width), jnp.bfloat16),
            pltpu.VMEM((tokens, depth), jnp.bfloat16),
            pltpu.VMEM((parts, rows // parts, depth), jnp.bfloat16),
            pltpu.VMEM((depth, tokens), jnp.bfloat16),
            pltpu.VMEM((heads, tokens, 4 * HD), jnp.bfloat16),
            pltpu.SemaphoreType.DMA((4 + parts,)),
            pltpu.SemaphoreType.DMA((parts,)),
        ],
        compiler_params=BIG,
        cost_estimate=cost(2 * tokens * rows * depth, 12 * MIB),
        name="pack",
    )(q, k, v, g, w)


def rows_of(parts):
    return parts[0] if len(parts) == 1 else jnp.concatenate(parts, axis=0)


def cols_of(parts):
    return parts[0] if len(parts) == 1 else jnp.concatenate(parts, axis=1)


def attention_kernel(
    place_ref, ids_ref, count_ref, order_ref, in_ref,
    grad_ref, near_ref, ahead_ref, behind_ref, across_ref, kt_ref, vt_ref, att_ref, acc_ref,
):
    blocks = in_ref.shape[0]
    for j in range(blocks):
        kt_ref[j] = in_ref[j, :, HD : 2 * HD].T
        vt_ref[j] = in_ref[j, :, 2 * HD : 3 * HD].T
    acc_ref[...] = jnp.zeros_like(acc_ref)

    def step(at, carry):
        members = [order_ref[at * GROUP + g] for g in range(GROUP)]

        def live(n):
            slots = [[ids_ref[i, s] for s in range(n)] for i in members]
            qs = [in_ref[i, :, 0:HD] for i in members]
            cts = [in_ref[i, :, 3 * HD : 4 * HD] for i in members]
            cs = [ct.T for ct in cts]
            scores = [
                dot(rows_of([in_ref[j, :, HD : 2 * HD] for j in js]), q.T)
                for js, q in zip(slots, qs)
            ]
            cots = [
                dot(rows_of([in_ref[j, :, 2 * HD : 3 * HD] for j in js]), ct)
                for js, ct in zip(slots, cts)
            ]
            for g in range(1, GROUP):
                count = count_ref[members[g]]
                scores[g] = rows_of(
                    [
                        scores[g][s * BLK : (s + 1) * BLK] + jnp.where(s < count, 0.0, NEG_FILL)
                        for s in range(n)
                    ]
                )
            peaks = [jnp.max(s, axis=0, keepdims=True) for s in scores]
            weights = [jnp.exp2((s - m) * (SCALE * LOG2E)) for s, m in zip(scores, peaks)]
            probs = [w * (1.0 / jnp.sum(w, axis=0, keepdims=True)) for w in weights]
            lows = [p.astype(jnp.bfloat16) for p in probs]
            deltas = [
                jnp.sum(low.astype(jnp.float32) * c, axis=0, keepdims=True)
                for low, c in zip(lows, cots)
            ]
            terms = [
                (p * ((c - d) * SCALE)).astype(jnp.bfloat16)
                for p, c, d in zip(probs, cots, deltas)
            ]
            for js, term, low, q, c in zip(slots, terms, lows, qs, cs):
                key_part = dot(term, q)
                value_part = dot(low, c)
                for s, j in enumerate(js):
                    acc_ref[j, :, :HD] += key_part[s * BLK : (s + 1) * BLK]
                    acc_ref[j, :, HD:] += value_part[s * BLK : (s + 1) * BLK]
            for i, js, term, low in zip(members, slots, terms, lows):
                query_part = dot(cols_of([kt_ref[j] for j in js]), term)
                grad_ref[i, :, 0:HD] = query_part.astype(jnp.bfloat16).T
                att = dot(cols_of([vt_ref[j] for j in js]), low)
                att_ref[i] = att.astype(jnp.bfloat16)

        top = count_ref[members[0]]
        for n in range(1, ids_ref.shape[1] + 1):
            pl.when(top == n)(functools.partial(live, n))
        return carry

    lax.fori_loop(0, blocks // GROUP, step, 0)
    for j in range(blocks):
        grad_ref[j, :, HD : 3 * HD] = acc_ref[j].astype(jnp.bfloat16)
    for out_ref, hops in zip((near_ref, ahead_ref, behind_ref, across_ref), HOPS):
        out_ref[...] = att_ref[pl.ds(lax.rem(place_ref[0] + hops, SIDE) * SIDE, SIDE)]


def attention_backward(place, ids, count, order, rows):
    blocks = rows.shape[0]
    turned = pltpu.VMEM((blocks, HD, BLK), jnp.bfloat16)
    return pl.pallas_call(
        attention_kernel,
        in_specs=[SMEM] * 4 + [VMEM],
        out_specs=[VMEM] * 5,
        out_shape=[shaped(blocks, BLK, 3 * HD)] + [shaped(SIDE, HD, BLK)] * 4,
        scratch_shapes=[turned, turned, turned, pltpu.VMEM((blocks, BLK, 2 * HD), jnp.float32)],
        compiler_params=MEDIUM,
        cost_estimate=cost(2 * 5 * 128 * 128**3, 4 * MIB, 2**21),
        name="attention_backward",
    )(place, ids, count, order, rows)


def by_count(count):
    at = jnp.arange(count.shape[0], dtype=jnp.int32)
    level = count[None, :] == count[:, None]
    ahead = (count[None, :] > count[:, None]) | (level & (at[None, :] < at[:, None]))
    rank = jnp.sum(ahead.astype(jnp.int32), axis=1)
    return jnp.sum(jnp.where(rank[None, :] == at[:, None], at[None, :], 0), axis=1)


def unpack_kernel(in_ref, q_ref, k_ref, v_ref):
    for h in range(in_ref.shape[0]):
        cols = slice(h * HD, (h + 1) * HD)
        q_ref[:, cols] = in_ref[h, :, 0:HD]
        k_ref[:, cols] = in_ref[h, :, HD : 2 * HD]
        v_ref[:, cols] = in_ref[h, :, 2 * HD : 3 * HD]


def unpack(rows, steps=2):
    heads, tokens, _ = rows.shape
    part = pl.BlockSpec((tokens, heads * HD // steps), lambda i: (0, i))
    return pl.pallas_call(
        unpack_kernel,
        grid=(steps,),
        in_specs=[pl.BlockSpec((heads // steps, tokens, 3 * HD), lambda i: (i, 0, 0))],
        out_specs=[part] * 3,
        out_shape=[shaped(tokens, heads * HD)] * 3,
        compiler_params=BIG,
        cost_estimate=cost(0, 3 * MIB),
        name="unpack",
    )(rows)


def weight_kernel(place_ref, a0, a1, a2, a3, *refs):
    pieces, (keep_own, keep_rest, give_own, give_rest, lhs_ref) = refs[:-5], refs[-5:]
    half = HD // 2

    @pl.when(pl.program_id(0) == 0)
    def _():
        core, x = place_ref[1], place_ref[2]
        for n, hops in enumerate(HOPS):
            block = lax.rem(x + SIDE - hops, SIDE)
            for head, att in enumerate((a0, a1, a2, a3)):
                for side in range(2):
                    rows = att[block, pl.ds(lax.rem(core + side, 2) * half, half), :]
                    at = (side * SIDE + head) * half
                    lhs_ref[at : at + half, n * BLK : (n + 1) * BLK] = rows

    rhs = jnp.concatenate([piece[...] for piece in pieces], axis=0)
    res = dot(lhs_ref[...], rhs).astype(jnp.bfloat16)
    for side, (own, rest) in enumerate(((keep_own, keep_rest), (give_own, give_rest))):
        at = side * SIDE * half
        own[...] = res[at : at + half]
        for n in range(SIDE - 1):
            rest[n] = res[at + (n + 1) * half : at + (n + 2) * half]


def weight_part(place, atts, pieces, steps=2):
    width = pieces[0].shape[1]
    half = HD // 2
    cols = width // steps
    att = pl.BlockSpec(atts[0].shape, lambda i: (0, 0, 0))
    own = pl.BlockSpec((half, cols), lambda i: (0, i))
    rest = pl.BlockSpec((SIDE - 1, half, cols), lambda i: (0, 0, i))
    return pl.pallas_call(
        weight_kernel,
        grid=(steps,),
        in_specs=[SMEM] + [att] * SIDE
        + [pl.BlockSpec((piece.shape[0], cols), lambda i: (0, i)) for piece in pieces],
        out_specs=[own, rest] * 2,
        out_shape=[shaped(half, width), shaped(SIDE - 1, half, width)] * 2,
        scratch_shapes=[pltpu.VMEM((2 * SIDE * half, SIDE * BLK), jnp.bfloat16)],
        compiler_params=SMALL,
        cost_estimate=cost(2 * 512 * 512 * 2048, 5 * MIB),
        name="weight_part",
    )(place, *atts, *pieces)


def assemble_kernel(scale, place_ref, kept, given, *refs):
    out_ref = refs[-1]
    half = kept.shape[0]
    for side, rows in enumerate((kept, given)):
        first = lax.rem(place_ref[1] + side, 2) * half
        out_ref[pl.ds(pl.multiple_of(first, half), half), :] = rows[...].astype(jnp.float32) * scale


def assemble(place, kept, given, scale, rest):
    return pl.pallas_call(
        functools.partial(assemble_kernel, scale),
        in_specs=[SMEM, VMEM, VMEM] + [ANY] * len(rest),
        out_specs=VMEM,
        out_shape=shaped(HD, kept.shape[1], dtype=jnp.float32),
        compiler_params=SMALL,
        cost_estimate=cost(0, 2 * MIB),
        name="assemble",
    )(place, kept, given, *rest)


def shift_x(a, d):
    return lax.ppermute(a, "seq", [(s, s // SIDE * SIDE + (s + d) % SIDE) for s in range(SIDE**2)])


def shift_z(a, d):
    return lax.ppermute(a, "seq", [(s, (s + d * SIDE) % SIDE**2) for s in range(SIDE**2)])


def shift_y(a, d):
    return lax.ppermute(a, "dp", [(s, (s + 2 * d) % 8) for s in range(8)])


def sibling(a):
    return lax.ppermute(a, "dp", [(s, s ^ 1) for s in range(8)])


def wide(a):
    return a.astype(jnp.float32)


def on_device(saved_query, saved_key, saved_value, out_grad, out_weight, block_index, block_count):
    seq_at = lax.axis_index("seq")
    core = lax.axis_index("dp") % 2
    z, x = seq_at // SIDE, seq_at % SIDE
    ids, count = block_index[0], block_count[0]
    place = jnp.stack([z, core, x]).astype(jnp.int32)

    def by_seq(a):
        return lax.all_to_all(a, "seq", split_axis=0, concat_axis=0, tiled=True)

    packed = pack(saved_query[0], saved_key[0], saved_value[0], out_grad[0], out_weight)
    rows = by_seq(packed)
    pieces = [out_grad[0]] + [shift_x(out_grad[0], d) for d in HOPS[1:]]

    grads, near, *rest = attention_backward(place, ids, count, by_count(count), rows)
    atts = [near] + [shift_z(a, d) for a, d in zip(rest, HOPS[1:])]
    token_grads = unpack(by_seq(grads))

    keep_own, keep_rest, give_own, give_rest = weight_part(place, atts, pieces)
    theirs = (wide(keep_rest) + wide(sibling(give_rest))).astype(jnp.bfloat16)
    row = wide(keep_own) + wide(sibling(give_own))
    for n, d in enumerate(HOPS[1:]):
        row = row + wide(shift_z(theirs[n], -d))
    row = row.astype(jnp.bfloat16)
    ahead, behind, across = shift_y(row, 1), shift_y(row, -1), shift_y(row, 2)
    total = ((wide(row) + wide(across)) + (wide(ahead) + wide(behind))).astype(jnp.bfloat16)
    weight_scale = (BLK * SIDE**2 * 8) ** (-0.5)
    weight_grad = assemble(place, total, sibling(total), weight_scale, token_grads[:DEPS])
    return *(grad[None] for grad in token_grads), weight_grad


def solution(mesh):
    placed = P("dp", "seq", None)
    return jax.shard_map(
        on_device,
        mesh=mesh,
        in_specs=(placed, placed, placed, placed, P(), P("dp", None, None), P("dp", None)),
        out_specs=(placed, placed, placed, P("seq", None)),
        check_vma=False,
    )
```

```python
import functools

import jax
import jax.numpy as jnp
from jax import lax
from jax.experimental import pallas as pl
from jax.experimental.pallas import tpu as pltpu
from jax.sharding import PartitionSpec as P

HD = 128
BLK = 128
SIDE = 4
GROUP = 4
HOPS = (0, 1, 3, 2)
NEG_FILL = -1e30
LOG2E = 1.4426950408889634
SCALE = HD**-0.5
MIB = 2**20
BIG = pltpu.CompilerParams(vmem_limit_bytes=60 * MIB)
MEDIUM = pltpu.CompilerParams(vmem_limit_bytes=32 * MIB)
SMALL = pltpu.CompilerParams(vmem_limit_bytes=16 * MIB)
VMEM = pl.BlockSpec(memory_space=pltpu.VMEM)
ANY = pl.BlockSpec(memory_space=pl.ANY)
SMEM = pl.BlockSpec(memory_space=pltpu.SMEM)
NN = (((1,), (0,)), ((), ()))


def dot(a, b, dims=NN):
    return lax.dot_general(a, b, dims, preferred_element_type=jnp.float32)


def cost(flops, size, exps=0):
    return pl.CostEstimate(flops=flops, bytes_accessed=size, transcendentals=exps)


def shaped(*dims, dtype=jnp.bfloat16):
    return jax.ShapeDtypeStruct(dims, dtype)


def pack_kernel(q, k, v, g, w, out, q_in, k_in, v_in, g_in, w_in, turned, packed, sems, done):
    parts, height, _ = w_in.shape
    heads = packed.shape[0] // parts
    loads = [
        pltpu.make_async_copy(src, dst, sems.at[n])
        for n, (src, dst) in enumerate(((g, g_in), (q, q_in), (k, k_in), (v, v_in)))
    ]
    loads += [
        pltpu.make_async_copy(w.at[pl.ds(p * height, height)], w_in.at[p], sems.at[4 + p])
        for p in range(parts)
    ]
    for load in loads:
        load.start()
    loads[0].wait()
    for n in range(g_in.shape[1] // BLK):
        turned[n * BLK : (n + 1) * BLK, :] = g_in[:, n * BLK : (n + 1) * BLK].T
    for load in loads[1:4]:
        load.wait()
    for h in range(packed.shape[0]):
        cols = slice(h * HD, (h + 1) * HD)
        packed[h, :, 0:HD] = q_in[:, cols]
        packed[h, :, HD : 2 * HD] = k_in[:, cols]
        packed[h, :, 2 * HD : 3 * HD] = v_in[:, cols]
    stores = []
    for p in range(parts):
        loads[4 + p].wait()
        cot = dot(w_in[p], turned[...]).astype(jnp.bfloat16)
        for n in range(heads):
            packed[p * heads + n, :, 3 * HD : 4 * HD] = cot[n * HD : (n + 1) * HD]
        some = pl.ds(p * heads, heads)
        stores.append(pltpu.make_async_copy(packed.at[some], out.at[some], done.at[p]))
        stores[-1].start()
    for store in stores:
        store.wait()


def pack(q, k, v, g, w, parts=8):
    tokens, width = q.shape
    rows, depth = w.shape
    heads = rows // HD
    return pl.pallas_call(
        pack_kernel,
        in_specs=[ANY] * 5,
        out_specs=ANY,
        out_shape=shaped(heads, tokens, 4 * HD),
        scratch_shapes=[
            pltpu.VMEM((tokens, width), jnp.bfloat16),
            pltpu.VMEM((tokens, width), jnp.bfloat16),
            pltpu.VMEM((tokens, width), jnp.bfloat16),
            pltpu.VMEM((tokens, depth), jnp.bfloat16),
            pltpu.VMEM((parts, rows // parts, depth), jnp.bfloat16),
            pltpu.VMEM((depth, tokens), jnp.bfloat16),
            pltpu.VMEM((heads, tokens, 4 * HD), jnp.bfloat16),
            pltpu.SemaphoreType.DMA((4 + parts,)),
            pltpu.SemaphoreType.DMA((parts,)),
        ],
        compiler_params=BIG,
        cost_estimate=cost(2 * tokens * rows * depth, 12 * MIB),
        name="pack",
    )(q, k, v, g, w)


def rows_of(parts):
    return parts[0] if len(parts) == 1 else jnp.concatenate(parts, axis=0)


def cols_of(parts):
    return parts[0] if len(parts) == 1 else jnp.concatenate(parts, axis=1)


def live_scores(scores, count_ref, members, n):
    out = scores[:1]
    for s, member in zip(scores[1:], members[1:]):
        count = count_ref[member]
        out.append(
            rows_of(
                [
                    s[c * BLK : (c + 1) * BLK] + jnp.where(c < count, 0.0, NEG_FILL)
                    for c in range(n)
                ]
            )
        )
    return out


def each_step(blocks, count_ref, order_ref, slots, live):
    def step(at, carry):
        members = [order_ref[at * GROUP + g] for g in range(GROUP)]
        top = count_ref[members[0]]
        for n in range(1, slots + 1):
            pl.when(top == n)(functools.partial(live, members, n))
        return carry

    lax.fori_loop(0, blocks // GROUP, step, 0)


def forward_kernel(
    ids_ref, count_ref, order_ref, in_ref, att_ref, norm_ref, vt_ref
):
    blocks = in_ref.shape[0]
    for j in range(blocks):
        vt_ref[j] = in_ref[j, :, 2 * HD : 3 * HD].T

    def live(members, n):
        slots = [[ids_ref[i, s] for s in range(n)] for i in members]
        scores = [
            dot(rows_of([in_ref[j, :, HD : 2 * HD] for j in js]), in_ref[i, :, 0:HD].T)
            for i, js in zip(members, slots)
        ]
        scores = live_scores(scores, count_ref, members, n)
        peaks = [jnp.max(s, axis=0, keepdims=True) for s in scores]
        weights = [jnp.exp2((s - m) * (SCALE * LOG2E)) for s, m in zip(scores, peaks)]
        inverses = [1.0 / jnp.sum(w, axis=0, keepdims=True) for w in weights]
        lows = [(w * v).astype(jnp.bfloat16) for w, v in zip(weights, inverses)]
        for i, js, low, peak, inverse in zip(members, slots, lows, peaks, inverses):
            att = dot(cols_of([vt_ref[j] for j in js]), low)
            att_ref[i] = att.astype(jnp.bfloat16)
            norm_ref[i, 0:1, :] = peak
            norm_ref[i, 1:2, :] = inverse

    each_step(blocks, count_ref, order_ref, ids_ref.shape[1], live)


def attention_forward(ids, count, order, rows):
    blocks = rows.shape[0]
    return pl.pallas_call(
        forward_kernel,
        in_specs=[SMEM] * 3 + [VMEM],
        out_specs=[VMEM] * 2,
        out_shape=[shaped(blocks, HD, BLK), shaped(blocks, 8, BLK, dtype=jnp.float32)],
        scratch_shapes=[pltpu.VMEM((blocks, HD, BLK), jnp.bfloat16)],
        compiler_params=MEDIUM,
        cost_estimate=cost(2 * 2 * 128 * 128**3, 3 * MIB, 2**21),
        name="attention_forward",
    )(ids, count, order, rows)


def backward_kernel(
    ids_ref, count_ref, order_ref, in_ref, norm_ref, grad_ref, mark_ref, kt_ref, acc_ref
):
    blocks = in_ref.shape[0]
    for j in range(blocks):
        kt_ref[j] = in_ref[j, :, HD : 2 * HD].T
    acc_ref[...] = jnp.zeros_like(acc_ref)
    zero = jnp.zeros((HD, BLK), jnp.bfloat16)

    def live(members, n):
        slots = [[ids_ref[i, s] for s in range(n)] for i in members]
        qs = [in_ref[i, :, 0:HD] for i in members]
        cts = [in_ref[i, :, 3 * HD : 4 * HD] for i in members]
        both = [
            dot(
                rows_of([in_ref[j, :, HD : 3 * HD] for j in js]),
                rows_of([cols_of([q.T, zero]), cols_of([zero, ct])]),
            )
            for js, q, ct in zip(slots, qs, cts)
        ]
        scores = live_scores([b[:, :BLK] for b in both], count_ref, members, n)
        cots = [b[:, BLK:] for b in both]
        probs = [
            jnp.exp2((s - norm_ref[i, 0:1, :]) * (SCALE * LOG2E)) * norm_ref[i, 1:2, :]
            for s, i in zip(scores, members)
        ]
        lows = [p.astype(jnp.bfloat16) for p in probs]
        deltas = [
            jnp.sum(low.astype(jnp.float32) * c, axis=0, keepdims=True)
            for low, c in zip(lows, cots)
        ]
        terms = [
            (p * ((c - d) * SCALE)).astype(jnp.bfloat16)
            for p, c, d in zip(probs, cots, deltas)
        ]
        for js, term, low, q, ct in zip(slots, terms, lows, qs, cts):
            key_part = dot(term, q)
            value_part = dot(low, ct.T)
            for s, j in enumerate(js):
                acc_ref[j, :, :HD] += key_part[s * BLK : (s + 1) * BLK]
                acc_ref[j, :, HD:] += value_part[s * BLK : (s + 1) * BLK]
        for i, js, term in zip(members, slots, terms):
            query_part = dot(cols_of([kt_ref[j] for j in js]), term)
            grad_ref[i, :, 0:HD] = query_part.astype(jnp.bfloat16).T

    each_step(blocks, count_ref, order_ref, ids_ref.shape[1], live)
    for j in range(blocks):
        grad_ref[j, :, HD : 3 * HD] = acc_ref[j].astype(jnp.bfloat16)
    mark_ref[...] = norm_ref[0]


def attention_backward(ids, count, order, rows, norms):
    blocks = rows.shape[0]
    return pl.pallas_call(
        backward_kernel,
        in_specs=[SMEM] * 3 + [VMEM] * 2,
        out_specs=[VMEM] * 2,
        out_shape=[shaped(blocks, BLK, 3 * HD), shaped(*norms.shape[1:], dtype=jnp.float32)],
        scratch_shapes=[
            pltpu.VMEM((blocks, HD, BLK), jnp.bfloat16),
            pltpu.VMEM((blocks, BLK, 2 * HD), jnp.float32),
        ],
        compiler_params=MEDIUM,
        cost_estimate=cost(2 * 5 * 128 * 128**3, 4 * MIB, 2**21),
        name="attention_backward",
    )(ids, count, order, rows, norms)


def by_count(count):
    at = jnp.arange(count.shape[0], dtype=jnp.int32)
    level = count[None, :] == count[:, None]
    ahead = (count[None, :] > count[:, None]) | (level & (at[None, :] < at[:, None]))
    rank = jnp.sum(ahead.astype(jnp.int32), axis=1)
    return jnp.sum(jnp.where(rank[None, :] == at[:, None], at[None, :], 0), axis=1)


def unpack_kernel(in_ref, q, k, v, rows_ref, sems):
    stores = []
    for n, out in enumerate((q, k, v)):
        for h in range(in_ref.shape[0]):
            rows_ref[n, :, h * HD : (h + 1) * HD] = in_ref[h, :, n * HD : (n + 1) * HD]
        stores.append(pltpu.make_async_copy(rows_ref.at[n], out, sems.at[n]))
        stores[-1].start()
    for store in stores:
        store.wait()


def unpack(rows):
    heads, tokens, _ = rows.shape
    return pl.pallas_call(
        unpack_kernel,
        in_specs=[VMEM],
        out_specs=[pl.BlockSpec(memory_space=pltpu.HBM)] * 3,
        out_shape=[shaped(tokens, heads * HD)] * 3,
        scratch_shapes=[
            pltpu.VMEM((3, tokens, heads * HD), jnp.bfloat16),
            pltpu.SemaphoreType.DMA((3,)),
        ],
        compiler_params=SMALL,
        cost_estimate=cost(0, 3 * MIB),
        name="unpack",
    )(rows)


def weight_kernel(place_ref, mark_ref, att_ref, *refs):
    pieces, (keep_own, keep_rest, give_own, give_rest, lhs_ref) = refs[:-5], refs[-5:]
    half = HD // 2

    @pl.when(pl.program_id(0) == 0)
    def _():
        z, core, x = place_ref[0], place_ref[1], place_ref[2]
        for n, hops in enumerate(HOPS):
            block = lax.rem(x + SIDE - hops, SIDE)
            for head, back in enumerate(HOPS):
                at_z = lax.rem(z + SIDE - back, SIDE)
                for side in range(2):
                    rows = att_ref[at_z, block, pl.ds(lax.rem(core + side, 2) * half, half), :]
                    at = (side * SIDE + head) * half
                    lhs_ref[at : at + half, n * BLK : (n + 1) * BLK] = rows

    rhs = jnp.concatenate([piece[...] for piece in pieces], axis=0)
    res = dot(lhs_ref[...], rhs).astype(jnp.bfloat16)
    for side, (own, rest) in enumerate(((keep_own, keep_rest), (give_own, give_rest))):
        at = side * SIDE * half
        own[...] = res[at : at + half]
        for n in range(SIDE - 1):
            rest[n] = res[at + (n + 1) * half : at + (n + 2) * half]


def weight_part(place, mark, atts, pieces, steps=2):
    width = pieces[0].shape[1]
    half = HD // 2
    cols = width // steps
    att = pl.BlockSpec(atts.shape, lambda i: (0, 0, 0, 0))
    own = pl.BlockSpec((half, cols), lambda i: (0, i))
    rest = pl.BlockSpec((SIDE - 1, half, cols), lambda i: (0, 0, i))
    return pl.pallas_call(
        weight_kernel,
        grid=(steps,),
        in_specs=[SMEM, ANY, att]
        + [pl.BlockSpec((piece.shape[0], cols), lambda i: (0, i)) for piece in pieces],
        out_specs=[own, rest] * 2,
        out_shape=[shaped(half, width), shaped(SIDE - 1, half, width)] * 2,
        scratch_shapes=[pltpu.VMEM((2 * SIDE * half, SIDE * BLK), jnp.bfloat16)],
        compiler_params=SMALL,
        cost_estimate=cost(2 * 512 * 512 * 2048, 5 * MIB),
        name="weight_part",
    )(place, mark, atts, *pieces)


def assemble_kernel(scale, place_ref, kept, given, *refs):
    out_ref = refs[-1]
    half = kept.shape[0]
    for side, rows in enumerate((kept, given)):
        first = lax.rem(place_ref[1] + side, 2) * half
        out_ref[pl.ds(pl.multiple_of(first, half), half), :] = rows[...].astype(jnp.float32) * scale


def assemble(place, kept, given, scale, rest):
    return pl.pallas_call(
        functools.partial(assemble_kernel, scale),
        in_specs=[SMEM, VMEM, VMEM] + [ANY] * len(rest),
        out_specs=VMEM,
        out_shape=shaped(HD, kept.shape[1], dtype=jnp.float32),
        compiler_params=SMALL,
        cost_estimate=cost(0, 2 * MIB),
        name="assemble",
    )(place, kept, given, *rest)


def shift_x(a, d):
    return lax.ppermute(a, "seq", [(s, s // SIDE * SIDE + (s + d) % SIDE) for s in range(SIDE**2)])


def shift_z(a, d):
    return lax.ppermute(a, "seq", [(s, (s + d * SIDE) % SIDE**2) for s in range(SIDE**2)])


def shift_y(a, d):
    return lax.ppermute(a, "dp", [(s, (s + 2 * d) % 8) for s in range(8)])


def sibling(a):
    return lax.ppermute(a, "dp", [(s, s ^ 1) for s in range(8)])


def wide(a):
    return a.astype(jnp.float32)


def on_device(saved_query, saved_key, saved_value, out_grad, out_weight, block_index, block_count):
    seq_at = lax.axis_index("seq")
    core = lax.axis_index("dp") % 2
    z, x = seq_at // SIDE, seq_at % SIDE
    ids, count = block_index[0], block_count[0]
    place = jnp.stack([z, core, x]).astype(jnp.int32)

    def by_seq(a):
        return lax.all_to_all(a, "seq", split_axis=0, concat_axis=0, tiled=True)

    packed = pack(saved_query[0], saved_key[0], saved_value[0], out_grad[0], out_weight)
    rows = by_seq(packed)
    pieces = [out_grad[0]] + [shift_x(out_grad[0], d) for d in HOPS[1:]]

    order = by_count(count)
    attention, norms = attention_forward(ids, count, order, rows)
    atts = lax.all_to_all(
        attention.reshape(SIDE, SIDE, HD, BLK),
        "seq",
        split_axis=0,
        concat_axis=0,
        axis_index_groups=[[i * SIDE + n for i in range(SIDE)] for n in range(SIDE)],
        tiled=True,
    )
    grads, mark = attention_backward(ids, count, order, rows, norms)

    token_grads = unpack(by_seq(grads))

    keep_own, keep_rest, give_own, give_rest = weight_part(place, mark, atts, pieces)
    theirs = (wide(keep_rest) + wide(sibling(give_rest))).astype(jnp.bfloat16)
    row = wide(keep_own) + wide(sibling(give_own))
    for n, d in enumerate(HOPS[1:]):
        row = row + wide(shift_z(theirs[n], -d))
    row = row.astype(jnp.bfloat16)
    ahead, behind, across = shift_y(row, 1), shift_y(row, -1), shift_y(row, 2)
    total = ((wide(row) + wide(across)) + (wide(ahead) + wide(behind))).astype(jnp.bfloat16)
    weight_scale = (BLK * SIDE**2 * 8) ** (-0.5)
    weight_grad = assemble(place, total, sibling(total), weight_scale, token_grads[:1])
    return *(grad[None] for grad in token_grads), weight_grad


def solution(mesh):
    placed = P("dp", "seq", None)
    return jax.shard_map(
        on_device,
        mesh=mesh,
        in_specs=(placed, placed, placed, placed, P(), P("dp", None, None), P("dp", None)),
        out_specs=(placed, placed, placed, P("seq", None)),
        check_vma=False,
    )
```

```python
import functools

import jax
import jax.numpy as jnp
from jax import lax
from jax.experimental import pallas as pl
from jax.experimental.pallas import tpu as pltpu
from jax.sharding import PartitionSpec as P

HD = 128
BLK = 128
SIDE = 4
GROUP = 4
HOPS = (0, 1, 3, 2)
NEG_FILL = -1e30
LOG2E = 1.4426950408889634
SCALE = HD**-0.5
MIB = 2**20
BIG = pltpu.CompilerParams(vmem_limit_bytes=60 * MIB)
MEDIUM = pltpu.CompilerParams(vmem_limit_bytes=32 * MIB)
SMALL = pltpu.CompilerParams(vmem_limit_bytes=16 * MIB)
VMEM = pl.BlockSpec(memory_space=pltpu.VMEM)
ANY = pl.BlockSpec(memory_space=pl.ANY)
SMEM = pl.BlockSpec(memory_space=pltpu.SMEM)
NN = (((1,), (0,)), ((), ()))


def dot(a, b, dims=NN):
    return lax.dot_general(a, b, dims, preferred_element_type=jnp.float32)


def cost(flops, size, exps=0):
    return pl.CostEstimate(flops=flops, bytes_accessed=size, transcendentals=exps)


def shaped(*dims, dtype=jnp.bfloat16):
    return jax.ShapeDtypeStruct(dims, dtype)


def pack_kernel(q, k, v, g, w, out, q_in, k_in, v_in, g_in, w_in, turned, packed, sems, done):
    parts, height, _ = w_in.shape
    heads = packed.shape[0] // parts
    loads = [
        pltpu.make_async_copy(src, dst, sems.at[n])
        for n, (src, dst) in enumerate(((g, g_in), (q, q_in), (k, k_in), (v, v_in)))
    ]
    loads += [
        pltpu.make_async_copy(w.at[pl.ds(p * height, height)], w_in.at[p], sems.at[4 + p])
        for p in range(parts)
    ]
    for load in loads:
        load.start()
    loads[0].wait()
    for n in range(g_in.shape[1] // BLK):
        turned[n * BLK : (n + 1) * BLK, :] = g_in[:, n * BLK : (n + 1) * BLK].T
    for load in loads[1:4]:
        load.wait()
    for h in range(packed.shape[0]):
        cols = slice(h * HD, (h + 1) * HD)
        packed[h, :, 0:HD] = q_in[:, cols]
        packed[h, :, HD : 2 * HD] = k_in[:, cols]
        packed[h, :, 2 * HD : 3 * HD] = v_in[:, cols]
    stores = []
    for p in range(parts):
        loads[4 + p].wait()
        cot = dot(w_in[p], turned[...]).astype(jnp.bfloat16)
        for n in range(heads):
            packed[p * heads + n, :, 3 * HD : 4 * HD] = cot[n * HD : (n + 1) * HD]
        some = pl.ds(p * heads, heads)
        stores.append(pltpu.make_async_copy(packed.at[some], out.at[some], done.at[p]))
        stores[-1].start()
    for store in stores:
        store.wait()


def pack(q, k, v, g, w, parts=8):
    tokens, width = q.shape
    rows, depth = w.shape
    heads = rows // HD
    return pl.pallas_call(
        pack_kernel,
        in_specs=[ANY] * 5,
        out_specs=ANY,
        out_shape=shaped(heads, tokens, 4 * HD),
        scratch_shapes=[
            pltpu.VMEM((tokens, width), jnp.bfloat16),
            pltpu.VMEM((tokens, width), jnp.bfloat16),
            pltpu.VMEM((tokens, width), jnp.bfloat16),
            pltpu.VMEM((tokens, depth), jnp.bfloat16),
            pltpu.VMEM((parts, rows // parts, depth), jnp.bfloat16),
            pltpu.VMEM((depth, tokens), jnp.bfloat16),
            pltpu.VMEM((heads, tokens, 4 * HD), jnp.bfloat16),
            pltpu.SemaphoreType.DMA((4 + parts,)),
            pltpu.SemaphoreType.DMA((parts,)),
        ],
        compiler_params=BIG,
        cost_estimate=cost(2 * tokens * rows * depth, 12 * MIB),
        name="pack",
    )(q, k, v, g, w)


def rows_of(parts):
    return parts[0] if len(parts) == 1 else jnp.concatenate(parts, axis=0)


def cols_of(parts):
    return parts[0] if len(parts) == 1 else jnp.concatenate(parts, axis=1)


def live_scores(scores, count_ref, members, n):
    out = scores[:1]
    for s, member in zip(scores[1:], members[1:]):
        count = count_ref[member]
        out.append(
            rows_of(
                [
                    s[c * BLK : (c + 1) * BLK] + jnp.where(c < count, 0.0, NEG_FILL)
                    for c in range(n)
                ]
            )
        )
    return out


def each_step(blocks, count_ref, order_ref, slots, live):
    def step(at, carry):
        members = [order_ref[at * GROUP + g] for g in range(GROUP)]
        top = count_ref[members[0]]
        for n in range(1, slots + 1):
            pl.when(top == n)(functools.partial(live, members, n))
        return carry

    lax.fori_loop(0, blocks // GROUP, step, 0)


def forward_kernel(
    ids_ref, count_ref, order_ref, in_ref, att_ref, norm_ref, vt_ref
):
    blocks = in_ref.shape[0]
    for j in range(blocks):
        vt_ref[j] = in_ref[j, :, 2 * HD : 3 * HD].T

    def live(members, n):
        slots = [[ids_ref[i, s] for s in range(n)] for i in members]
        scores = [
            dot(rows_of([in_ref[j, :, HD : 2 * HD] for j in js]), in_ref[i, :, 0:HD].T)
            for i, js in zip(members, slots)
        ]
        scores = live_scores(scores, count_ref, members, n)
        peaks = [jnp.max(s, axis=0, keepdims=True) for s in scores]
        weights = [jnp.exp2((s - m) * (SCALE * LOG2E)) for s, m in zip(scores, peaks)]
        inverses = [1.0 / jnp.sum(w, axis=0, keepdims=True) for w in weights]
        lows = [(w * v).astype(jnp.bfloat16) for w, v in zip(weights, inverses)]
        for i, js, low, peak, inverse in zip(members, slots, lows, peaks, inverses):
            att = dot(cols_of([vt_ref[j] for j in js]), low)
            att_ref[i] = att.astype(jnp.bfloat16)
            norm_ref[i, 0:1, :] = peak
            norm_ref[i, 1:2, :] = inverse

    each_step(blocks, count_ref, order_ref, ids_ref.shape[1], live)


def attention_forward(ids, count, order, rows):
    blocks = rows.shape[0]
    return pl.pallas_call(
        forward_kernel,
        in_specs=[SMEM] * 3 + [VMEM],
        out_specs=[VMEM] * 2,
        out_shape=[shaped(blocks, HD, BLK), shaped(blocks, 8, BLK, dtype=jnp.float32)],
        scratch_shapes=[pltpu.VMEM((blocks, HD, BLK), jnp.bfloat16)],
        compiler_params=MEDIUM,
        cost_estimate=cost(2 * 2 * 128 * 128**3, 3 * MIB, 2**21),
        name="attention_forward",
    )(ids, count, order, rows)


def backward_kernel(
    ids_ref, count_ref, order_ref, in_ref, norm_ref, grad_ref, mark_ref, kt_ref, acc_ref
):
    blocks = in_ref.shape[0]
    for j in range(blocks):
        kt_ref[j] = in_ref[j, :, HD : 2 * HD].T
    acc_ref[...] = jnp.zeros_like(acc_ref)
    zero = jnp.zeros((HD, BLK), jnp.bfloat16)

    def live(members, n):
        slots = [[ids_ref[i, s] for s in range(n)] for i in members]
        qs = [in_ref[i, :, 0:HD] for i in members]
        cts = [in_ref[i, :, 3 * HD : 4 * HD] for i in members]
        both = [
            dot(
                rows_of([in_ref[j, :, HD : 3 * HD] for j in js]),
                rows_of([cols_of([q.T, zero]), cols_of([zero, ct])]),
            )
            for js, q, ct in zip(slots, qs, cts)
        ]
        scores = live_scores([b[:, :BLK] for b in both], count_ref, members, n)
        cots = [b[:, BLK:] for b in both]
        probs = [
            jnp.exp2((s - norm_ref[i, 0:1, :]) * (SCALE * LOG2E)) * norm_ref[i, 1:2, :]
            for s, i in zip(scores, members)
        ]
        lows = [p.astype(jnp.bfloat16) for p in probs]
        deltas = [
            jnp.sum(low.astype(jnp.float32) * c, axis=0, keepdims=True)
            for low, c in zip(lows, cots)
        ]
        terms = [
            (p * ((c - d) * SCALE)).astype(jnp.bfloat16)
            for p, c, d in zip(probs, cots, deltas)
        ]
        for js, term, low, q, ct in zip(slots, terms, lows, qs, cts):
            key_part = dot(term, q)
            value_part = dot(low, ct.T)
            for s, j in enumerate(js):
                acc_ref[j, :, :HD] += key_part[s * BLK : (s + 1) * BLK]
                acc_ref[j, :, HD:] += value_part[s * BLK : (s + 1) * BLK]
        for i, js, term in zip(members, slots, terms):
            query_part = dot(cols_of([kt_ref[j] for j in js]), term)
            grad_ref[i, :, 0:HD] = query_part.astype(jnp.bfloat16).T

    each_step(blocks, count_ref, order_ref, ids_ref.shape[1], live)
    for j in range(blocks):
        grad_ref[j, :, HD : 3 * HD] = acc_ref[j].astype(jnp.bfloat16)
    mark_ref[...] = norm_ref[0]


def attention_backward(ids, count, order, rows, norms):
    blocks = rows.shape[0]
    return pl.pallas_call(
        backward_kernel,
        in_specs=[SMEM] * 3 + [VMEM] * 2,
        out_specs=[VMEM] * 2,
        out_shape=[shaped(blocks, BLK, 3 * HD), shaped(*norms.shape[1:], dtype=jnp.float32)],
        scratch_shapes=[
            pltpu.VMEM((blocks, HD, BLK), jnp.bfloat16),
            pltpu.VMEM((blocks, BLK, 2 * HD), jnp.float32),
        ],
        compiler_params=MEDIUM,
        cost_estimate=cost(2 * 5 * 128 * 128**3, 4 * MIB, 2**21),
        name="attention_backward",
    )(ids, count, order, rows, norms)


def by_count(count):
    at = jnp.arange(count.shape[0], dtype=jnp.int32)
    level = count[None, :] == count[:, None]
    ahead = (count[None, :] > count[:, None]) | (level & (at[None, :] < at[:, None]))
    rank = jnp.sum(ahead.astype(jnp.int32), axis=1)
    return jnp.sum(jnp.where(rank[None, :] == at[:, None], at[None, :], 0), axis=1)


def unpack_kernel(in_ref, q, k, v, rows_ref, sems):
    stores = []
    for n, out in enumerate((q, k, v)):
        for h in range(in_ref.shape[0]):
            rows_ref[n, :, h * HD : (h + 1) * HD] = in_ref[h, :, n * HD : (n + 1) * HD]
        stores.append(pltpu.make_async_copy(rows_ref.at[n], out, sems.at[n]))
        stores[-1].start()
    for store in stores:
        store.wait()


def unpack(rows):
    heads, tokens, _ = rows.shape
    return pl.pallas_call(
        unpack_kernel,
        in_specs=[VMEM],
        out_specs=[pl.BlockSpec(memory_space=pltpu.HBM)] * 3,
        out_shape=[shaped(tokens, heads * HD)] * 3,
        scratch_shapes=[
            pltpu.VMEM((3, tokens, heads * HD), jnp.bfloat16),
            pltpu.SemaphoreType.DMA((3,)),
        ],
        compiler_params=SMALL,
        cost_estimate=cost(0, 3 * MIB),
        name="unpack",
    )(rows)


def weight_kernel(place_ref, mark_ref, att_ref, *refs):
    pieces, (keep_own, keep_rest, give_own, give_rest, lhs_ref) = refs[:-5], refs[-5:]
    half = HD // 2

    @pl.when(pl.program_id(0) == 0)
    def _():
        z, core, x = place_ref[0], place_ref[1], place_ref[2]
        for n, hops in enumerate(HOPS):
            block = lax.rem(x + SIDE - hops, SIDE)
            for head, back in enumerate(HOPS):
                at_z = lax.rem(z + SIDE - back, SIDE)
                for side in range(2):
                    rows = att_ref[at_z, block, pl.ds(lax.rem(core + side, 2) * half, half), :]
                    at = (side * SIDE + head) * half
                    lhs_ref[at : at + half, n * BLK : (n + 1) * BLK] = rows

    rhs = jnp.concatenate([piece[...] for piece in pieces], axis=0)
    res = dot(lhs_ref[...], rhs).astype(jnp.bfloat16)
    for side, (own, rest) in enumerate(((keep_own, keep_rest), (give_own, give_rest))):
        at = side * SIDE * half
        own[...] = res[at : at + half]
        for n in range(SIDE - 1):
            rest[n] = res[at + (n + 1) * half : at + (n + 2) * half]


def weight_part(place, mark, atts, pieces, steps=2):
    width = pieces[0].shape[1]
    half = HD // 2
    cols = width // steps
    att = pl.BlockSpec(atts.shape, lambda i: (0, 0, 0, 0))
    own = pl.BlockSpec((half, cols), lambda i: (0, i))
    rest = pl.BlockSpec((SIDE - 1, half, cols), lambda i: (0, 0, i))
    return pl.pallas_call(
        weight_kernel,
        grid=(steps,),
        in_specs=[SMEM, ANY, att]
        + [pl.BlockSpec((piece.shape[0], cols), lambda i: (0, i)) for piece in pieces],
        out_specs=[own, rest] * 2,
        out_shape=[shaped(half, width), shaped(SIDE - 1, half, width)] * 2,
        scratch_shapes=[pltpu.VMEM((2 * SIDE * half, SIDE * BLK), jnp.bfloat16)],
        compiler_params=SMALL,
        cost_estimate=cost(2 * 512 * 512 * 2048, 5 * MIB),
        name="weight_part",
    )(place, mark, atts, *pieces)


def assemble_kernel(scale, place_ref, kept, given, out_ref):
    half = kept.shape[0]
    for side, rows in enumerate((kept, given)):
        first = lax.rem(place_ref[1] + side, 2) * half
        out_ref[pl.ds(pl.multiple_of(first, half), half), :] = rows[...].astype(jnp.float32) * scale


def assemble(place, kept, given, scale):
    return pl.pallas_call(
        functools.partial(assemble_kernel, scale),
        in_specs=[SMEM, VMEM, VMEM],
        out_specs=VMEM,
        out_shape=shaped(HD, kept.shape[1], dtype=jnp.float32),
        compiler_params=SMALL,
        cost_estimate=cost(0, 2 * MIB),
        name="assemble",
    )(place, kept, given)


def after(a, other):
    return pl.pallas_call(
        lambda *refs: None,
        in_specs=[ANY, ANY],
        out_specs=ANY,
        out_shape=shaped(*a.shape),
        input_output_aliases={0: 0},
        compiler_params=SMALL,
        cost_estimate=cost(0, 0),
        name="after",
    )(a, other)


def shift_x(a, d):
    return lax.ppermute(a, "seq", [(s, s // SIDE * SIDE + (s + d) % SIDE) for s in range(SIDE**2)])


def shift_z(a, d):
    return lax.ppermute(a, "seq", [(s, (s + d * SIDE) % SIDE**2) for s in range(SIDE**2)])


def shift_y(a, d):
    return lax.ppermute(a, "dp", [(s, (s + 2 * d) % 8) for s in range(8)])


def sibling(a):
    return lax.ppermute(a, "dp", [(s, s ^ 1) for s in range(8)])


def wide(a):
    return a.astype(jnp.float32)


def on_device(saved_query, saved_key, saved_value, out_grad, out_weight, block_index, block_count):
    seq_at = lax.axis_index("seq")
    core = lax.axis_index("dp") % 2
    z, x = seq_at // SIDE, seq_at % SIDE
    ids, count = block_index[0], block_count[0]
    place = jnp.stack([z, core, x]).astype(jnp.int32)

    def by_seq(a):
        return lax.all_to_all(a, "seq", split_axis=0, concat_axis=0, tiled=True)

    packed = pack(saved_query[0], saved_key[0], saved_value[0], out_grad[0], out_weight)
    rows = by_seq(packed)
    pieces = [out_grad[0]] + [shift_x(out_grad[0], d) for d in HOPS[1:]]

    order = by_count(count)
    attention, norms = attention_forward(ids, count, order, rows)
    atts = lax.all_to_all(
        attention.reshape(SIDE, SIDE, HD, BLK),
        "seq",
        split_axis=0,
        concat_axis=0,
        axis_index_groups=[[i * SIDE + n for i in range(SIDE)] for n in range(SIDE)],
        tiled=True,
    )
    grads, mark = attention_backward(ids, count, order, rows, norms)

    keep_own, keep_rest, give_own, give_rest = weight_part(place, mark, atts, pieces)
    given = sibling(give_rest)
    theirs = [(wide(keep_rest[n]) + wide(given[n])).astype(jnp.bfloat16) for n in range(SIDE - 1)]
    sent = [shift_z(rows, -d) for rows, d in zip(theirs, HOPS[1:])]
    token_grads = unpack(by_seq(after(grads, sent[0][:16, :128])))
    row = wide(keep_own) + wide(sibling(give_own))
    for rows in sent:
        row = row + wide(rows)
    row = row.astype(jnp.bfloat16)
    ahead, behind, across = shift_y(row, 1), shift_y(row, -1), shift_y(row, 2)
    total = ((wide(row) + wide(across)) + (wide(ahead) + wide(behind))).astype(jnp.bfloat16)
    weight_scale = (BLK * SIDE**2 * 8) ** (-0.5)
    weight_grad = assemble(place, total, sibling(total), weight_scale)
    return *(grad[None] for grad in token_grads), weight_grad


def solution(mesh):
    placed = P("dp", "seq", None)
    return jax.shard_map(
        on_device,
        mesh=mesh,
        in_specs=(placed, placed, placed, placed, P(), P("dp", None, None), P("dp", None)),
        out_specs=(placed, placed, placed, P("seq", None)),
        check_vma=False,
    )
```

```python
import functools

import jax
import jax.numpy as jnp
from jax import lax
from jax.experimental import pallas as pl
from jax.experimental.pallas import tpu as pltpu
from jax.sharding import PartitionSpec as P

HD = 128
BLK = 128
SIDE = 4
GROUP = 4
HOPS = (0, 1, 3, 2)
NEG_FILL = -1e30
LOG2E = 1.4426950408889634
SCALE = HD**-0.5
MIB = 2**20
BIG = pltpu.CompilerParams(vmem_limit_bytes=60 * MIB)
MEDIUM = pltpu.CompilerParams(vmem_limit_bytes=32 * MIB)
SMALL = pltpu.CompilerParams(vmem_limit_bytes=16 * MIB)
VMEM = pl.BlockSpec(memory_space=pltpu.VMEM)
ANY = pl.BlockSpec(memory_space=pl.ANY)
SMEM = pl.BlockSpec(memory_space=pltpu.SMEM)
NN = (((1,), (0,)), ((), ()))


def dot(a, b, dims=NN):
    return lax.dot_general(a, b, dims, preferred_element_type=jnp.float32)


def cost(flops, size, exps=0):
    return pl.CostEstimate(flops=flops, bytes_accessed=size, transcendentals=exps)


def shaped(*dims, dtype=jnp.bfloat16):
    return jax.ShapeDtypeStruct(dims, dtype)


def pack_kernel(q, k, v, g, w, out, q_in, k_in, v_in, g_in, w_in, turned, packed, sems, done):
    parts, height, _ = w_in.shape
    heads = packed.shape[0] // parts
    loads = [
        pltpu.make_async_copy(src, dst, sems.at[n])
        for n, (src, dst) in enumerate(((g, g_in), (q, q_in), (k, k_in), (v, v_in)))
    ]
    loads += [
        pltpu.make_async_copy(w.at[pl.ds(p * height, height)], w_in.at[p], sems.at[4 + p])
        for p in range(parts)
    ]
    for load in loads:
        load.start()
    loads[0].wait()
    for n in range(g_in.shape[1] // BLK):
        turned[n * BLK : (n + 1) * BLK, :] = g_in[:, n * BLK : (n + 1) * BLK].T
    for load in loads[1:4]:
        load.wait()
    for h in range(packed.shape[0]):
        cols = slice(h * HD, (h + 1) * HD)
        packed[h, :, 0:HD] = q_in[:, cols]
        packed[h, :, HD : 2 * HD] = k_in[:, cols]
        packed[h, :, 2 * HD : 3 * HD] = v_in[:, cols]
    stores = []
    for p in range(parts):
        loads[4 + p].wait()
        cot = dot(w_in[p], turned[...]).astype(jnp.bfloat16)
        for n in range(heads):
            packed[p * heads + n, :, 3 * HD : 4 * HD] = cot[n * HD : (n + 1) * HD]
        some = pl.ds(p * heads, heads)
        stores.append(pltpu.make_async_copy(packed.at[some], out.at[some], done.at[p]))
        stores[-1].start()
    for store in stores:
        store.wait()


def pack(q, k, v, g, w, parts=8):
    tokens, width = q.shape
    rows, depth = w.shape
    heads = rows // HD
    return pl.pallas_call(
        pack_kernel,
        in_specs=[ANY] * 5,
        out_specs=ANY,
        out_shape=shaped(heads, tokens, 4 * HD),
        scratch_shapes=[
            pltpu.VMEM((tokens, width), jnp.bfloat16),
            pltpu.VMEM((tokens, width), jnp.bfloat16),
            pltpu.VMEM((tokens, width), jnp.bfloat16),
            pltpu.VMEM((tokens, depth), jnp.bfloat16),
            pltpu.VMEM((parts, rows // parts, depth), jnp.bfloat16),
            pltpu.VMEM((depth, tokens), jnp.bfloat16),
            pltpu.VMEM((heads, tokens, 4 * HD), jnp.bfloat16),
            pltpu.SemaphoreType.DMA((4 + parts,)),
            pltpu.SemaphoreType.DMA((parts,)),
        ],
        compiler_params=BIG,
        cost_estimate=cost(2 * tokens * rows * depth, 12 * MIB),
        name="pack",
    )(q, k, v, g, w)


def rows_of(parts):
    return parts[0] if len(parts) == 1 else jnp.concatenate(parts, axis=0)


def cols_of(parts):
    return parts[0] if len(parts) == 1 else jnp.concatenate(parts, axis=1)


def live_scores(scores, count_ref, members, n):
    out = scores[:1]
    for s, member in zip(scores[1:], members[1:]):
        count = count_ref[member]
        out.append(
            rows_of(
                [
                    s[c * BLK : (c + 1) * BLK] + jnp.where(c < count, 0.0, NEG_FILL)
                    for c in range(n)
                ]
            )
        )
    return out


def each_step(blocks, count_ref, order_ref, slots, live):
    def step(at, carry):
        members = [order_ref[at * GROUP + g] for g in range(GROUP)]
        top = count_ref[members[0]]
        for n in range(1, slots + 1):
            pl.when(top == n)(functools.partial(live, members, n))
        return carry

    lax.fori_loop(0, blocks // GROUP, step, 0)


def forward_kernel(
    ids_ref, count_ref, order_ref, in_ref, att_ref, norm_ref, vt_ref
):
    blocks = in_ref.shape[0]
    for j in range(blocks):
        vt_ref[j] = in_ref[j, :, 2 * HD : 3 * HD].T

    def live(members, n):
        slots = [[ids_ref[i, s] for s in range(n)] for i in members]
        scores = [
            dot(rows_of([in_ref[j, :, HD : 2 * HD] for j in js]), in_ref[i, :, 0:HD].T)
            for i, js in zip(members, slots)
        ]
        scores = live_scores(scores, count_ref, members, n)
        peaks = [jnp.max(s, axis=0, keepdims=True) for s in scores]
        weights = [jnp.exp2((s - m) * (SCALE * LOG2E)) for s, m in zip(scores, peaks)]
        inverses = [1.0 / jnp.sum(w, axis=0, keepdims=True) for w in weights]
        lows = [(w * v).astype(jnp.bfloat16) for w, v in zip(weights, inverses)]
        for i, js, low, peak, inverse in zip(members, slots, lows, peaks, inverses):
            att = dot(cols_of([vt_ref[j] for j in js]), low)
            att_ref[i] = att.astype(jnp.bfloat16)
            norm_ref[i, 0:1, :] = peak
            norm_ref[i, 1:2, :] = inverse

    each_step(blocks, count_ref, order_ref, ids_ref.shape[1], live)


def attention_forward(ids, count, order, rows):
    blocks = rows.shape[0]
    return pl.pallas_call(
        forward_kernel,
        in_specs=[SMEM] * 3 + [VMEM],
        out_specs=[VMEM] * 2,
        out_shape=[shaped(blocks, HD, BLK), shaped(blocks, 8, BLK, dtype=jnp.float32)],
        scratch_shapes=[pltpu.VMEM((blocks, HD, BLK), jnp.bfloat16)],
        compiler_params=MEDIUM,
        cost_estimate=cost(2 * 2 * 128 * 128**3, 3 * MIB, 2**21),
        name="attention_forward",
    )(ids, count, order, rows)


def backward_kernel(
    ids_ref, count_ref, order_ref, in_ref, norm_ref, grad_ref, mark_ref, kt_ref, acc_ref
):
    blocks = in_ref.shape[0]
    for j in range(blocks):
        kt_ref[j] = in_ref[j, :, HD : 2 * HD].T
    acc_ref[...] = jnp.zeros_like(acc_ref)
    zero = jnp.zeros((HD, BLK), jnp.bfloat16)

    def live(members, n):
        slots = [[ids_ref[i, s] for s in range(n)] for i in members]
        qs = [in_ref[i, :, 0:HD] for i in members]
        cts = [in_ref[i, :, 3 * HD : 4 * HD] for i in members]
        both = [
            dot(
                rows_of([in_ref[j, :, HD : 3 * HD] for j in js]),
                rows_of([cols_of([q.T, zero]), cols_of([zero, ct])]),
            )
            for js, q, ct in zip(slots, qs, cts)
        ]
        scores = live_scores([b[:, :BLK] for b in both], count_ref, members, n)
        cots = [b[:, BLK:] for b in both]
        probs = [
            jnp.exp2((s - norm_ref[i, 0:1, :]) * (SCALE * LOG2E)) * norm_ref[i, 1:2, :]
            for s, i in zip(scores, members)
        ]
        lows = [p.astype(jnp.bfloat16) for p in probs]
        deltas = [
            jnp.sum(low.astype(jnp.float32) * c, axis=0, keepdims=True)
            for low, c in zip(lows, cots)
        ]
        terms = [
            (p * ((c - d) * SCALE)).astype(jnp.bfloat16)
            for p, c, d in zip(probs, cots, deltas)
        ]
        for js, term, low, q, ct in zip(slots, terms, lows, qs, cts):
            key_part = dot(term, q)
            value_part = dot(low, ct.T)
            for s, j in enumerate(js):
                acc_ref[j, :, :HD] += key_part[s * BLK : (s + 1) * BLK]
                acc_ref[j, :, HD:] += value_part[s * BLK : (s + 1) * BLK]
        for i, js, term in zip(members, slots, terms):
            query_part = dot(cols_of([kt_ref[j] for j in js]), term)
            grad_ref[i, :, 0:HD] = query_part.astype(jnp.bfloat16).T

    each_step(blocks, count_ref, order_ref, ids_ref.shape[1], live)
    for j in range(blocks):
        grad_ref[j, :, HD : 3 * HD] = acc_ref[j].astype(jnp.bfloat16)
    mark_ref[...] = norm_ref[0]


def attention_backward(ids, count, order, rows, norms):
    blocks = rows.shape[0]
    return pl.pallas_call(
        backward_kernel,
        in_specs=[SMEM] * 3 + [VMEM] * 2,
        out_specs=[VMEM] * 2,
        out_shape=[shaped(blocks, BLK, 3 * HD), shaped(*norms.shape[1:], dtype=jnp.float32)],
        scratch_shapes=[
            pltpu.VMEM((blocks, HD, BLK), jnp.bfloat16),
            pltpu.VMEM((blocks, BLK, 2 * HD), jnp.float32),
        ],
        compiler_params=MEDIUM,
        cost_estimate=cost(2 * 5 * 128 * 128**3, 4 * MIB, 2**21),
        name="attention_backward",
    )(ids, count, order, rows, norms)


def by_count(count):
    at = jnp.arange(count.shape[0], dtype=jnp.int32)
    level = count[None, :] == count[:, None]
    ahead = (count[None, :] > count[:, None]) | (level & (at[None, :] < at[:, None]))
    rank = jnp.sum(ahead.astype(jnp.int32), axis=1)
    return jnp.sum(jnp.where(rank[None, :] == at[:, None], at[None, :], 0), axis=1)


def unpack_kernel(in_ref, q, k, v, rows_ref, sems):
    stores = []
    for n, out in enumerate((q, k, v)):
        for h in range(in_ref.shape[0]):
            rows_ref[n, :, h * HD : (h + 1) * HD] = in_ref[h, :, n * HD : (n + 1) * HD]
        stores.append(pltpu.make_async_copy(rows_ref.at[n], out, sems.at[n]))
        stores[-1].start()
    for store in stores:
        store.wait()


def unpack(rows):
    heads, tokens, _ = rows.shape
    return pl.pallas_call(
        unpack_kernel,
        in_specs=[VMEM],
        out_specs=[pl.BlockSpec(memory_space=pltpu.HBM)] * 3,
        out_shape=[shaped(tokens, heads * HD)] * 3,
        scratch_shapes=[
            pltpu.VMEM((3, tokens, heads * HD), jnp.bfloat16),
            pltpu.SemaphoreType.DMA((3,)),
        ],
        compiler_params=SMALL,
        cost_estimate=cost(0, 3 * MIB),
        name="unpack",
    )(rows)


def weight_kernel(side, place_ref, mark_ref, att_ref, *refs):
    pieces, (own, rest, lhs_ref) = refs[:-3], refs[-3:]
    half = HD // 2
    z, core, x = place_ref[0], place_ref[1], place_ref[2]
    first = pl.multiple_of(lax.rem(core + side, 2) * half, half)
    for n, hops in enumerate(HOPS):
        block = lax.rem(x + SIDE - hops, SIDE)
        for head, back in enumerate(HOPS):
            rows = att_ref[lax.rem(z + SIDE - back, SIDE), block, pl.ds(first, half), :]
            lhs_ref[head * half : (head + 1) * half, n * BLK : (n + 1) * BLK] = rows
    rhs = jnp.concatenate([piece[...] for piece in pieces], axis=0)
    res = dot(lhs_ref[...], rhs).astype(jnp.bfloat16)
    own[...] = res[:half]
    for n in range(SIDE - 1):
        rest[n] = res[(n + 1) * half : (n + 2) * half]


def weight_part(side, place, mark, atts, pieces):
    width = pieces[0].shape[1]
    half = HD // 2
    return pl.pallas_call(
        functools.partial(weight_kernel, side),
        in_specs=[SMEM, ANY] + [VMEM] * (1 + len(pieces)),
        out_specs=[VMEM, VMEM],
        out_shape=[shaped(half, width), shaped(SIDE - 1, half, width)],
        scratch_shapes=[pltpu.VMEM((SIDE * half, SIDE * BLK), jnp.bfloat16)],
        compiler_params=SMALL,
        cost_estimate=cost(2 * 256 * 512 * 2048, 4 * MIB),
        name="weight_part",
    )(place, mark, atts, *pieces)


def assemble_kernel(scale, place_ref, kept, given, out_ref):
    half = kept.shape[0]
    for side, rows in enumerate((kept, given)):
        first = lax.rem(place_ref[1] + side, 2) * half
        out_ref[pl.ds(pl.multiple_of(first, half), half), :] = rows[...].astype(jnp.float32) * scale


def assemble(place, kept, given, scale):
    return pl.pallas_call(
        functools.partial(assemble_kernel, scale),
        in_specs=[SMEM, VMEM, VMEM],
        out_specs=VMEM,
        out_shape=shaped(HD, kept.shape[1], dtype=jnp.float32),
        compiler_params=SMALL,
        cost_estimate=cost(0, 2 * MIB),
        name="assemble",
    )(place, kept, given)


def after(a, other):
    return pl.pallas_call(
        lambda *refs: None,
        in_specs=[ANY, ANY],
        out_specs=ANY,
        out_shape=shaped(*a.shape),
        input_output_aliases={0: 0},
        compiler_params=SMALL,
        cost_estimate=cost(0, 0),
        name="after",
    )(a, other)


def shift_x(a, d):
    return lax.ppermute(a, "seq", [(s, s // SIDE * SIDE + (s + d) % SIDE) for s in range(SIDE**2)])


def shift_z(a, d):
    return lax.ppermute(a, "seq", [(s, (s + d * SIDE) % SIDE**2) for s in range(SIDE**2)])


def shift_y(a, d):
    return lax.ppermute(a, "dp", [(s, (s + 2 * d) % 8) for s in range(8)])


def sibling(a):
    return lax.ppermute(a, "dp", [(s, s ^ 1) for s in range(8)])


def wide(a):
    return a.astype(jnp.float32)


def on_device(saved_query, saved_key, saved_value, out_grad, out_weight, block_index, block_count):
    seq_at = lax.axis_index("seq")
    core = lax.axis_index("dp") % 2
    z, x = seq_at // SIDE, seq_at % SIDE
    ids, count = block_index[0], block_count[0]
    place = jnp.stack([z, core, x]).astype(jnp.int32)

    def by_seq(a):
        return lax.all_to_all(a, "seq", split_axis=0, concat_axis=0, tiled=True)

    packed = pack(saved_query[0], saved_key[0], saved_value[0], out_grad[0], out_weight)
    rows = by_seq(packed)
    pieces = [out_grad[0]] + [shift_x(out_grad[0], d) for d in HOPS[1:]]

    order = by_count(count)
    attention, norms = attention_forward(ids, count, order, rows)
    atts = lax.all_to_all(
        attention.reshape(SIDE, SIDE, HD, BLK),
        "seq",
        split_axis=0,
        concat_axis=0,
        axis_index_groups=[[i * SIDE + n for i in range(SIDE)] for n in range(SIDE)],
        tiled=True,
    )
    grads, mark = attention_backward(ids, count, order, rows, norms)

    give_own, give_rest = weight_part(1, place, mark, atts, pieces)
    given = sibling(give_rest)
    keep_own, keep_rest = weight_part(0, place, mark, atts, pieces)
    theirs = [(wide(keep_rest[n]) + wide(given[n])).astype(jnp.bfloat16) for n in range(SIDE - 1)]
    sent = [shift_z(rows, -d) for rows, d in zip(theirs, HOPS[1:])]
    token_grads = unpack(by_seq(after(grads, sent[0][:16, :128])))
    row = wide(keep_own) + wide(sibling(give_own))
    for rows in sent:
        row = row + wide(rows)
    row = row.astype(jnp.bfloat16)
    ahead, behind, across = shift_y(row, 1), shift_y(row, -1), shift_y(row, 2)
    total = ((wide(row) + wide(across)) + (wide(ahead) + wide(behind))).astype(jnp.bfloat16)
    weight_scale = (BLK * SIDE**2 * 8) ** (-0.5)
    weight_grad = assemble(place, total, sibling(total), weight_scale)
    return *(grad[None] for grad in token_grads), weight_grad


def solution(mesh):
    placed = P("dp", "seq", None)
    return jax.shard_map(
        on_device,
        mesh=mesh,
        in_specs=(placed, placed, placed, placed, P(), P("dp", None, None), P("dp", None)),
        out_specs=(placed, placed, placed, P("seq", None)),
        check_vma=False,
    )
```

```python
import functools

import jax
import jax.numpy as jnp
from jax import lax
from jax.experimental import pallas as pl
from jax.experimental.pallas import tpu as pltpu
from jax.sharding import PartitionSpec as P

HD = 128
BLK = 128
SIDE = 4
GROUP = 4
HOPS = (0, 1, 3, 2)
NEG_FILL = -1e30
LOG2E = 1.4426950408889634
SCALE = HD**-0.5
MIB = 2**20
BIG = pltpu.CompilerParams(vmem_limit_bytes=60 * MIB)
MEDIUM = pltpu.CompilerParams(vmem_limit_bytes=32 * MIB)
SMALL = pltpu.CompilerParams(vmem_limit_bytes=16 * MIB)
VMEM = pl.BlockSpec(memory_space=pltpu.VMEM)
ANY = pl.BlockSpec(memory_space=pl.ANY)
SMEM = pl.BlockSpec(memory_space=pltpu.SMEM)
NN = (((1,), (0,)), ((), ()))


def dot(a, b, dims=NN):
    return lax.dot_general(a, b, dims, preferred_element_type=jnp.float32)


def cost(flops, size, exps=0):
    return pl.CostEstimate(flops=flops, bytes_accessed=size, transcendentals=exps)


def shaped(*dims, dtype=jnp.bfloat16):
    return jax.ShapeDtypeStruct(dims, dtype)


def pack_kernel(q, k, v, g, w, out, q_in, k_in, v_in, g_in, w_in, turned, packed, sems, done):
    parts, height, _ = w_in.shape
    heads = packed.shape[0] // parts
    loads = [
        pltpu.make_async_copy(src, dst, sems.at[n])
        for n, (src, dst) in enumerate(((g, g_in), (q, q_in), (k, k_in), (v, v_in)))
    ]
    loads += [
        pltpu.make_async_copy(w.at[pl.ds(p * height, height)], w_in.at[p], sems.at[4 + p])
        for p in range(parts)
    ]
    for load in loads:
        load.start()
    loads[0].wait()
    for n in range(g_in.shape[1] // BLK):
        turned[n * BLK : (n + 1) * BLK, :] = g_in[:, n * BLK : (n + 1) * BLK].T
    for load in loads[1:4]:
        load.wait()
    for h in range(packed.shape[0]):
        cols = slice(h * HD, (h + 1) * HD)
        packed[h, :, 0:HD] = q_in[:, cols]
        packed[h, :, HD : 2 * HD] = k_in[:, cols]
        packed[h, :, 2 * HD : 3 * HD] = v_in[:, cols]
    stores = []
    for p in range(parts):
        loads[4 + p].wait()
        cot = dot(w_in[p], turned[...]).astype(jnp.bfloat16)
        for n in range(heads):
            packed[p * heads + n, :, 3 * HD : 4 * HD] = cot[n * HD : (n + 1) * HD]
        some = pl.ds(p * heads, heads)
        stores.append(pltpu.make_async_copy(packed.at[some], out.at[some], done.at[p]))
        stores[-1].start()
    for store in stores:
        store.wait()


def pack(q, k, v, g, w, parts=8):
    tokens, width = q.shape
    rows, depth = w.shape
    heads = rows // HD
    return pl.pallas_call(
        pack_kernel,
        in_specs=[ANY] * 5,
        out_specs=ANY,
        out_shape=shaped(heads, tokens, 4 * HD),
        scratch_shapes=[
            pltpu.VMEM((tokens, width), jnp.bfloat16),
            pltpu.VMEM((tokens, width), jnp.bfloat16),
            pltpu.VMEM((tokens, width), jnp.bfloat16),
            pltpu.VMEM((tokens, depth), jnp.bfloat16),
            pltpu.VMEM((parts, rows // parts, depth), jnp.bfloat16),
            pltpu.VMEM((depth, tokens), jnp.bfloat16),
            pltpu.VMEM((heads, tokens, 4 * HD), jnp.bfloat16),
            pltpu.SemaphoreType.DMA((4 + parts,)),
            pltpu.SemaphoreType.DMA((parts,)),
        ],
        compiler_params=BIG,
        cost_estimate=cost(2 * tokens * rows * depth, 12 * MIB),
        name="pack",
    )(q, k, v, g, w)


def rows_of(parts):
    return parts[0] if len(parts) == 1 else jnp.concatenate(parts, axis=0)


def cols_of(parts):
    return parts[0] if len(parts) == 1 else jnp.concatenate(parts, axis=1)


def live_scores(scores, count_ref, members, n):
    out = scores[:1]
    for s, member in zip(scores[1:], members[1:]):
        count = count_ref[member]
        out.append(
            rows_of(
                [
                    s[c * BLK : (c + 1) * BLK] + jnp.where(c < count, 0.0, NEG_FILL)
                    for c in range(n)
                ]
            )
        )
    return out


def each_step(blocks, count_ref, order_ref, slots, live):
    def step(at, carry):
        members = [order_ref[at * GROUP + g] for g in range(GROUP)]
        top = count_ref[members[0]]
        for n in range(1, slots + 1):
            pl.when(top == n)(functools.partial(live, members, n))
        return carry

    lax.fori_loop(0, blocks // GROUP, step, 0)


def forward_kernel(
    ids_ref, count_ref, order_ref, in_ref, att_ref, norm_ref, vt_ref
):
    blocks = in_ref.shape[0]
    for j in range(blocks):
        vt_ref[j] = in_ref[j, :, 2 * HD : 3 * HD].T

    def live(members, n):
        slots = [[ids_ref[i, s] for s in range(n)] for i in members]
        scores = [
            dot(rows_of([in_ref[j, :, HD : 2 * HD] for j in js]), in_ref[i, :, 0:HD].T)
            for i, js in zip(members, slots)
        ]
        scores = live_scores(scores, count_ref, members, n)
        peaks = [jnp.max(s, axis=0, keepdims=True) for s in scores]
        weights = [jnp.exp2((s - m) * (SCALE * LOG2E)) for s, m in zip(scores, peaks)]
        inverses = [1.0 / jnp.sum(w, axis=0, keepdims=True) for w in weights]
        lows = [(w * v).astype(jnp.bfloat16) for w, v in zip(weights, inverses)]
        for i, js, low, peak, inverse in zip(members, slots, lows, peaks, inverses):
            att = dot(cols_of([vt_ref[j] for j in js]), low)
            att_ref[i] = att.astype(jnp.bfloat16)
            norm_ref[i, 0:1, :] = peak
            norm_ref[i, 1:2, :] = inverse

    each_step(blocks, count_ref, order_ref, ids_ref.shape[1], live)


def attention_forward(ids, count, order, rows):
    blocks = rows.shape[0]
    return pl.pallas_call(
        forward_kernel,
        in_specs=[SMEM] * 3 + [VMEM],
        out_specs=[VMEM] * 2,
        out_shape=[shaped(blocks, HD, BLK), shaped(blocks, 8, BLK, dtype=jnp.float32)],
        scratch_shapes=[pltpu.VMEM((blocks, HD, BLK), jnp.bfloat16)],
        compiler_params=MEDIUM,
        cost_estimate=cost(2 * 2 * 128 * 128**3, 3 * MIB, 2**21),
        name="attention_forward",
    )(ids, count, order, rows)


def backward_kernel(
    ids_ref, count_ref, order_ref, in_ref, norm_ref, grad_ref, mark_ref, kt_ref, acc_ref
):
    blocks = in_ref.shape[0]
    for j in range(blocks):
        kt_ref[j] = in_ref[j, :, HD : 2 * HD].T
    acc_ref[...] = jnp.zeros_like(acc_ref)
    zero = jnp.zeros((HD, BLK), jnp.bfloat16)

    def live(members, n):
        slots = [[ids_ref[i, s] for s in range(n)] for i in members]
        qs = [in_ref[i, :, 0:HD] for i in members]
        cts = [in_ref[i, :, 3 * HD : 4 * HD] for i in members]
        both = [
            dot(
                rows_of([in_ref[j, :, HD : 3 * HD] for j in js]),
                rows_of([cols_of([q.T, zero]), cols_of([zero, ct])]),
            )
            for js, q, ct in zip(slots, qs, cts)
        ]
        scores = live_scores([b[:, :BLK] for b in both], count_ref, members, n)
        cots = [b[:, BLK:] for b in both]
        probs = [
            jnp.exp2((s - norm_ref[i, 0:1, :]) * (SCALE * LOG2E)) * norm_ref[i, 1:2, :]
            for s, i in zip(scores, members)
        ]
        lows = [p.astype(jnp.bfloat16) for p in probs]
        deltas = [
            jnp.sum(low.astype(jnp.float32) * c, axis=0, keepdims=True)
            for low, c in zip(lows, cots)
        ]
        terms = [
            (p * ((c - d) * SCALE)).astype(jnp.bfloat16)
            for p, c, d in zip(probs, cots, deltas)
        ]
        for js, term, low, q, ct in zip(slots, terms, lows, qs, cts):
            key_part = dot(term, q)
            value_part = dot(low, ct.T)
            for s, j in enumerate(js):
                acc_ref[j, :, :HD] += key_part[s * BLK : (s + 1) * BLK]
                acc_ref[j, :, HD:] += value_part[s * BLK : (s + 1) * BLK]
        for i, js, term in zip(members, slots, terms):
            query_part = dot(cols_of([kt_ref[j] for j in js]), term)
            grad_ref[i, :, 0:HD] = query_part.astype(jnp.bfloat16).T

    each_step(blocks, count_ref, order_ref, ids_ref.shape[1], live)
    for j in range(blocks):
        grad_ref[j, :, HD : 3 * HD] = acc_ref[j].astype(jnp.bfloat16)
    mark_ref[...] = norm_ref[0]


def attention_backward(ids, count, order, rows, norms):
    blocks = rows.shape[0]
    return pl.pallas_call(
        backward_kernel,
        in_specs=[SMEM] * 3 + [VMEM] * 2,
        out_specs=[VMEM] * 2,
        out_shape=[shaped(blocks, BLK, 3 * HD), shaped(*norms.shape[1:], dtype=jnp.float32)],
        scratch_shapes=[
            pltpu.VMEM((blocks, HD, BLK), jnp.bfloat16),
            pltpu.VMEM((blocks, BLK, 2 * HD), jnp.float32),
        ],
        compiler_params=MEDIUM,
        cost_estimate=cost(2 * 5 * 128 * 128**3, 4 * MIB, 2**21),
        name="attention_backward",
    )(ids, count, order, rows, norms)


def by_count(count):
    at = jnp.arange(count.shape[0], dtype=jnp.int32)
    level = count[None, :] == count[:, None]
    ahead = (count[None, :] > count[:, None]) | (level & (at[None, :] < at[:, None]))
    rank = jnp.sum(ahead.astype(jnp.int32), axis=1)
    return jnp.sum(jnp.where(rank[None, :] == at[:, None], at[None, :], 0), axis=1)


def unpack_kernel(in_ref, q, k, v, rows_ref, sems):
    stores = []
    for n, out in enumerate((q, k, v)):
        for h in range(in_ref.shape[0]):
            rows_ref[n, :, h * HD : (h + 1) * HD] = in_ref[h, :, n * HD : (n + 1) * HD]
        stores.append(pltpu.make_async_copy(rows_ref.at[n], out, sems.at[n]))
        stores[-1].start()
    for store in stores:
        store.wait()


def unpack(rows):
    heads, tokens, _ = rows.shape
    return pl.pallas_call(
        unpack_kernel,
        in_specs=[VMEM],
        out_specs=[pl.BlockSpec(memory_space=pltpu.HBM)] * 3,
        out_shape=[shaped(tokens, heads * HD)] * 3,
        scratch_shapes=[
            pltpu.VMEM((3, tokens, heads * HD), jnp.bfloat16),
            pltpu.SemaphoreType.DMA((3,)),
        ],
        compiler_params=SMALL,
        cost_estimate=cost(0, 3 * MIB),
        name="unpack",
    )(rows)


def fill_rows(place_ref, att_ref, lhs_ref, side, top, hops):
    half = HD // 2
    z, core, x = place_ref[0], place_ref[1], place_ref[2]
    first = pl.multiple_of(lax.rem(core + side, 2) * half, half)
    for n, hop in enumerate(hops):
        block = lax.rem(x + SIDE - hop, SIDE)
        for head, back in enumerate(HOPS):
            rows = att_ref[lax.rem(z + SIDE - back, SIDE), block, pl.ds(first, half), :]
            at = top + head * half
            lhs_ref[at : at + half, n * BLK : (n + 1) * BLK] = rows


def weight_near_kernel(place_ref, mark_ref, att_ref, g0, g1, g2, keep, give, lhs_ref):
    height = keep.shape[0]
    for side in range(2):
        fill_rows(place_ref, att_ref, lhs_ref, side, side * height, HOPS[:-1])
    rhs = jnp.concatenate([g0[...], g1[...], g2[...]], axis=0)
    for side, out in enumerate((keep, give)):
        out[...] = dot(lhs_ref[side * height : (side + 1) * height], rhs)


def weight_near(place, mark, atts, pieces):
    width = pieces[0].shape[1]
    height = SIDE * HD // 2
    return pl.pallas_call(
        weight_near_kernel,
        in_specs=[SMEM, ANY] + [VMEM] * (1 + len(pieces)),
        out_specs=[VMEM, VMEM],
        out_shape=[shaped(height, width, dtype=jnp.float32)] * 2,
        scratch_shapes=[pltpu.VMEM((2 * height, len(pieces) * BLK), jnp.bfloat16)],
        compiler_params=SMALL,
        cost_estimate=cost(2 * 512 * 384 * 2048, 7 * MIB),
        name="weight_near",
    )(place, mark, atts, *pieces)


def weight_far_kernel(side, place_ref, att_ref, g3, near_ref, own, rest, lhs_ref):
    half = HD // 2
    fill_rows(place_ref, att_ref, lhs_ref, side, 0, HOPS[-1:])
    res = (near_ref[...] + dot(lhs_ref[...], g3[...])).astype(jnp.bfloat16)
    own[...] = res[:half]
    for n in range(SIDE - 1):
        rest[n] = res[(n + 1) * half : (n + 2) * half]


def weight_far(side, place, atts, piece, near):
    width = piece.shape[1]
    half = HD // 2
    return pl.pallas_call(
        functools.partial(weight_far_kernel, side),
        in_specs=[SMEM] + [VMEM] * 3,
        out_specs=[VMEM, VMEM],
        out_shape=[shaped(half, width), shaped(SIDE - 1, half, width)],
        scratch_shapes=[pltpu.VMEM((SIDE * half, BLK), jnp.bfloat16)],
        compiler_params=SMALL,
        cost_estimate=cost(2 * 256 * 128 * 2048, 4 * MIB),
        name="weight_far",
    )(place, atts, piece, near)


def assemble_kernel(scale, place_ref, kept, given, out_ref):
    half = kept.shape[0]
    for side, rows in enumerate((kept, given)):
        first = lax.rem(place_ref[1] + side, 2) * half
        out_ref[pl.ds(pl.multiple_of(first, half), half), :] = rows[...].astype(jnp.float32) * scale


def assemble(place, kept, given, scale):
    return pl.pallas_call(
        functools.partial(assemble_kernel, scale),
        in_specs=[SMEM, VMEM, VMEM],
        out_specs=VMEM,
        out_shape=shaped(HD, kept.shape[1], dtype=jnp.float32),
        compiler_params=SMALL,
        cost_estimate=cost(0, 2 * MIB),
        name="assemble",
    )(place, kept, given)


def after(a, other):
    return pl.pallas_call(
        lambda *refs: None,
        in_specs=[ANY, ANY],
        out_specs=ANY,
        out_shape=shaped(*a.shape),
        input_output_aliases={0: 0},
        compiler_params=SMALL,
        cost_estimate=cost(0, 0),
        name="after",
    )(a, other)


def shift_x(a, d):
    return lax.ppermute(a, "seq", [(s, s // SIDE * SIDE + (s + d) % SIDE) for s in range(SIDE**2)])


def shift_z(a, d):
    return lax.ppermute(a, "seq", [(s, (s + d * SIDE) % SIDE**2) for s in range(SIDE**2)])


def shift_y(a, d):
    return lax.ppermute(a, "dp", [(s, (s + 2 * d) % 8) for s in range(8)])


def sibling(a):
    return lax.ppermute(a, "dp", [(s, s ^ 1) for s in range(8)])


def wide(a):
    return a.astype(jnp.float32)


def on_device(saved_query, saved_key, saved_value, out_grad, out_weight, block_index, block_count):
    seq_at = lax.axis_index("seq")
    core = lax.axis_index("dp") % 2
    z, x = seq_at // SIDE, seq_at % SIDE
    ids, count = block_index[0], block_count[0]
    place = jnp.stack([z, core, x]).astype(jnp.int32)

    def by_seq(a):
        return lax.all_to_all(a, "seq", split_axis=0, concat_axis=0, tiled=True)

    packed = pack(saved_query[0], saved_key[0], saved_value[0], out_grad[0], out_weight)
    rows = by_seq(packed)
    pieces = [out_grad[0]] + [shift_x(out_grad[0], d) for d in HOPS[1:]]

    order = by_count(count)
    attention, norms = attention_forward(ids, count, order, rows)
    atts = lax.all_to_all(
        attention.reshape(SIDE, SIDE, HD, BLK),
        "seq",
        split_axis=0,
        concat_axis=0,
        axis_index_groups=[[i * SIDE + n for i in range(SIDE)] for n in range(SIDE)],
        tiled=True,
    )
    grads, mark = attention_backward(ids, count, order, rows, norms)

    near_keep, near_give = weight_near(place, mark, atts, pieces[:-1])
    give_own, give_rest = weight_far(1, place, atts, pieces[-1], near_give)
    given = sibling(give_rest)
    keep_own, keep_rest = weight_far(0, place, atts, pieces[-1], near_keep)
    theirs = [(wide(keep_rest[n]) + wide(given[n])).astype(jnp.bfloat16) for n in range(SIDE - 1)]
    sent = [shift_z(rows, -d) for rows, d in zip(theirs, HOPS[1:])]
    token_grads = unpack(by_seq(after(grads, sent[0][:16, :128])))
    row = wide(keep_own) + wide(sibling(give_own))
    for rows in sent:
        row = row + wide(rows)
    row = row.astype(jnp.bfloat16)
    ahead, behind, across = shift_y(row, 1), shift_y(row, -1), shift_y(row, 2)
    total = ((wide(row) + wide(across)) + (wide(ahead) + wide(behind))).astype(jnp.bfloat16)
    weight_scale = (BLK * SIDE**2 * 8) ** (-0.5)
    weight_grad = assemble(place, total, sibling(total), weight_scale)
    return *(grad[None] for grad in token_grads), weight_grad


def solution(mesh):
    placed = P("dp", "seq", None)
    return jax.shard_map(
        on_device,
        mesh=mesh,
        in_specs=(placed, placed, placed, placed, P(), P("dp", None, None), P("dp", None)),
        out_specs=(placed, placed, placed, P("seq", None)),
        check_vma=False,
    )
```

```python
import functools

import jax
import jax.numpy as jnp
from jax import lax
from jax.experimental import pallas as pl
from jax.experimental.pallas import tpu as pltpu
from jax.sharding import PartitionSpec as P

HD = 128
BLK = 128
SIDE = 4
GROUP = 4
HOPS = (0, 1, 3, 2)
NEG_FILL = -1e30
LOG2E = 1.4426950408889634
SCALE = HD**-0.5
MIB = 2**20
BIG = pltpu.CompilerParams(vmem_limit_bytes=60 * MIB)
MEDIUM = pltpu.CompilerParams(vmem_limit_bytes=32 * MIB)
SMALL = pltpu.CompilerParams(vmem_limit_bytes=16 * MIB)
VMEM = pl.BlockSpec(memory_space=pltpu.VMEM)
ANY = pl.BlockSpec(memory_space=pl.ANY)
SMEM = pl.BlockSpec(memory_space=pltpu.SMEM)
NN = (((1,), (0,)), ((), ()))


def dot(a, b, dims=NN):
    return lax.dot_general(a, b, dims, preferred_element_type=jnp.float32)


def cost(flops, size, exps=0):
    return pl.CostEstimate(flops=flops, bytes_accessed=size, transcendentals=exps)


def shaped(*dims, dtype=jnp.bfloat16):
    return jax.ShapeDtypeStruct(dims, dtype)


def pack_kernel(q, k, v, g, w, out, q_in, k_in, v_in, g_in, w_in, turned, packed, sems, done):
    parts, height, _ = w_in.shape
    heads = packed.shape[0] // parts
    loads = [
        pltpu.make_async_copy(src, dst, sems.at[n])
        for n, (src, dst) in enumerate(((g, g_in), (q, q_in), (k, k_in), (v, v_in)))
    ]
    loads += [
        pltpu.make_async_copy(w.at[pl.ds(p * height, height)], w_in.at[p], sems.at[4 + p])
        for p in range(parts)
    ]
    for load in loads:
        load.start()
    loads[0].wait()
    for n in range(g_in.shape[1] // BLK):
        turned[n * BLK : (n + 1) * BLK, :] = g_in[:, n * BLK : (n + 1) * BLK].T
    for load in loads[1:4]:
        load.wait()
    for h in range(packed.shape[0]):
        cols = slice(h * HD, (h + 1) * HD)
        packed[h, :, 0:HD] = q_in[:, cols]
        packed[h, :, HD : 2 * HD] = k_in[:, cols]
        packed[h, :, 2 * HD : 3 * HD] = v_in[:, cols]
    stores = []
    for p in range(parts):
        loads[4 + p].wait()
        cot = dot(w_in[p], turned[...]).astype(jnp.bfloat16)
        for n in range(heads):
            packed[p * heads + n, :, 3 * HD : 4 * HD] = cot[n * HD : (n + 1) * HD]
        some = pl.ds(p * heads, heads)
        stores.append(pltpu.make_async_copy(packed.at[some], out.at[some], done.at[p]))
        stores[-1].start()
    for store in stores:
        store.wait()


def pack(q, k, v, g, w, parts=8):
    tokens, width = q.shape
    rows, depth = w.shape
    heads = rows // HD
    return pl.pallas_call(
        pack_kernel,
        in_specs=[ANY] * 5,
        out_specs=ANY,
        out_shape=shaped(heads, tokens, 4 * HD),
        scratch_shapes=[
            pltpu.VMEM((tokens, width), jnp.bfloat16),
            pltpu.VMEM((tokens, width), jnp.bfloat16),
            pltpu.VMEM((tokens, width), jnp.bfloat16),
            pltpu.VMEM((tokens, depth), jnp.bfloat16),
            pltpu.VMEM((parts, rows // parts, depth), jnp.bfloat16),
            pltpu.VMEM((depth, tokens), jnp.bfloat16),
            pltpu.VMEM((heads, tokens, 4 * HD), jnp.bfloat16),
            pltpu.SemaphoreType.DMA((4 + parts,)),
            pltpu.SemaphoreType.DMA((parts,)),
        ],
        compiler_params=BIG,
        cost_estimate=cost(2 * tokens * rows * depth, 12 * MIB),
        name="pack",
    )(q, k, v, g, w)


def rows_of(parts):
    return parts[0] if len(parts) == 1 else jnp.concatenate(parts, axis=0)


def cols_of(parts):
    return parts[0] if len(parts) == 1 else jnp.concatenate(parts, axis=1)


def live_scores(scores, count_ref, members, n):
    out = scores[:1]
    for s, member in zip(scores[1:], members[1:]):
        count = count_ref[member]
        out.append(
            rows_of(
                [
                    s[c * BLK : (c + 1) * BLK] + jnp.where(c < count, 0.0, NEG_FILL)
                    for c in range(n)
                ]
            )
        )
    return out


def each_step(blocks, count_ref, order_ref, slots, live):
    def step(at, carry):
        members = [order_ref[at * GROUP + g] for g in range(GROUP)]
        top = count_ref[members[0]]
        for n in range(1, slots + 1):
            pl.when(top == n)(functools.partial(live, members, n))
        return carry

    lax.fori_loop(0, blocks // GROUP, step, 0)


def forward_kernel(
    ids_ref, count_ref, order_ref, in_ref, att_ref, norm_ref, vt_ref
):
    blocks = in_ref.shape[0]
    for j in range(blocks):
        vt_ref[j] = in_ref[j, :, 2 * HD : 3 * HD].T

    def live(members, n):
        slots = [[ids_ref[i, s] for s in range(n)] for i in members]
        scores = [
            dot(rows_of([in_ref[j, :, HD : 2 * HD] for j in js]), in_ref[i, :, 0:HD].T)
            for i, js in zip(members, slots)
        ]
        scores = live_scores(scores, count_ref, members, n)
        peaks = [jnp.max(s, axis=0, keepdims=True) for s in scores]
        weights = [jnp.exp2((s - m) * (SCALE * LOG2E)) for s, m in zip(scores, peaks)]
        inverses = [1.0 / jnp.sum(w, axis=0, keepdims=True) for w in weights]
        lows = [(w * v).astype(jnp.bfloat16) for w, v in zip(weights, inverses)]
        for i, js, low, peak, inverse in zip(members, slots, lows, peaks, inverses):
            att = dot(cols_of([vt_ref[j] for j in js]), low)
            att_ref[i] = att.astype(jnp.bfloat16)
            norm_ref[i, 0:1, :] = peak
            norm_ref[i, 1:2, :] = inverse

    each_step(blocks, count_ref, order_ref, ids_ref.shape[1], live)


def attention_forward(ids, count, order, rows):
    blocks = rows.shape[0]
    return pl.pallas_call(
        forward_kernel,
        in_specs=[SMEM] * 3 + [VMEM],
        out_specs=[VMEM] * 2,
        out_shape=[shaped(blocks, HD, BLK), shaped(blocks, 8, BLK, dtype=jnp.float32)],
        scratch_shapes=[pltpu.VMEM((blocks, HD, BLK), jnp.bfloat16)],
        compiler_params=MEDIUM,
        cost_estimate=cost(2 * 2 * 128 * 128**3, 3 * MIB, 2**21),
        name="attention_forward",
    )(ids, count, order, rows)


def backward_kernel(
    ids_ref, count_ref, order_ref, in_ref, norm_ref, grad_ref, mark_ref, kt_ref, acc_ref
):
    blocks = in_ref.shape[0]
    for j in range(blocks):
        kt_ref[j] = in_ref[j, :, HD : 2 * HD].T
    acc_ref[...] = jnp.zeros_like(acc_ref)
    zero = jnp.zeros((HD, BLK), jnp.bfloat16)

    def live(members, n):
        slots = [[ids_ref[i, s] for s in range(n)] for i in members]
        qs = [in_ref[i, :, 0:HD] for i in members]
        cts = [in_ref[i, :, 3 * HD : 4 * HD] for i in members]
        both = [
            dot(
                rows_of([in_ref[j, :, HD : 3 * HD] for j in js]),
                rows_of([cols_of([q.T, zero]), cols_of([zero, ct])]),
            )
            for js, q, ct in zip(slots, qs, cts)
        ]
        scores = live_scores([b[:, :BLK] for b in both], count_ref, members, n)
        cots = [b[:, BLK:] for b in both]
        probs = [
            jnp.exp2((s - norm_ref[i, 0:1, :]) * (SCALE * LOG2E)) * norm_ref[i, 1:2, :]
            for s, i in zip(scores, members)
        ]
        lows = [p.astype(jnp.bfloat16) for p in probs]
        deltas = [
            jnp.sum(low.astype(jnp.float32) * c, axis=0, keepdims=True)
            for low, c in zip(lows, cots)
        ]
        terms = [
            (p * ((c - d) * SCALE)).astype(jnp.bfloat16)
            for p, c, d in zip(probs, cots, deltas)
        ]
        for js, term, low, q, ct in zip(slots, terms, lows, qs, cts):
            key_part = dot(term, q)
            value_part = dot(low, ct.T)
            for s, j in enumerate(js):
                acc_ref[j, :, :HD] += key_part[s * BLK : (s + 1) * BLK]
                acc_ref[j, :, HD:] += value_part[s * BLK : (s + 1) * BLK]
        for i, js, term in zip(members, slots, terms):
            query_part = dot(cols_of([kt_ref[j] for j in js]), term)
            grad_ref[i, :, 0:HD] = query_part.astype(jnp.bfloat16).T

    each_step(blocks, count_ref, order_ref, ids_ref.shape[1], live)
    for j in range(blocks):
        grad_ref[j, :, HD : 3 * HD] = acc_ref[j].astype(jnp.bfloat16)
    mark_ref[...] = norm_ref[0]


def attention_backward(ids, count, order, rows, norms):
    blocks = rows.shape[0]
    return pl.pallas_call(
        backward_kernel,
        in_specs=[SMEM] * 3 + [VMEM] * 2,
        out_specs=[VMEM] * 2,
        out_shape=[shaped(blocks, BLK, 3 * HD), shaped(*norms.shape[1:], dtype=jnp.float32)],
        scratch_shapes=[
            pltpu.VMEM((blocks, HD, BLK), jnp.bfloat16),
            pltpu.VMEM((blocks, BLK, 2 * HD), jnp.float32),
        ],
        compiler_params=MEDIUM,
        cost_estimate=cost(2 * 5 * 128 * 128**3, 4 * MIB, 2**21),
        name="attention_backward",
    )(ids, count, order, rows, norms)


def by_count(count):
    at = jnp.arange(count.shape[0], dtype=jnp.int32)
    level = count[None, :] == count[:, None]
    ahead = (count[None, :] > count[:, None]) | (level & (at[None, :] < at[:, None]))
    rank = jnp.sum(ahead.astype(jnp.int32), axis=1)
    return jnp.sum(jnp.where(rank[None, :] == at[:, None], at[None, :], 0), axis=1)


def unpack_kernel(in_ref, q, k, v, rows_ref, sems):
    stores = []
    for n, out in enumerate((q, k, v)):
        for h in range(in_ref.shape[0]):
            rows_ref[n, :, h * HD : (h + 1) * HD] = in_ref[h, :, n * HD : (n + 1) * HD]
        stores.append(pltpu.make_async_copy(rows_ref.at[n], out, sems.at[n]))
        stores[-1].start()
    for store in stores:
        store.wait()


def unpack(rows):
    heads, tokens, _ = rows.shape
    return pl.pallas_call(
        unpack_kernel,
        in_specs=[VMEM],
        out_specs=[pl.BlockSpec(memory_space=pltpu.HBM)] * 3,
        out_shape=[shaped(tokens, heads * HD)] * 3,
        scratch_shapes=[
            pltpu.VMEM((3, tokens, heads * HD), jnp.bfloat16),
            pltpu.SemaphoreType.DMA((3,)),
        ],
        compiler_params=SMALL,
        cost_estimate=cost(0, 3 * MIB),
        name="unpack",
    )(rows)


def weight_kernel(side, place_ref, mark_ref, att_ref, *refs):
    pieces, (own, rest, lhs_ref) = refs[:-3], refs[-3:]
    half = HD // 2
    z, core, x = place_ref[0], place_ref[1], place_ref[2]
    first = pl.multiple_of(lax.rem(core + side, 2) * half, half)
    for n, hops in enumerate(HOPS):
        block = lax.rem(x + SIDE - hops, SIDE)
        for head, back in enumerate(HOPS):
            rows = att_ref[lax.rem(z + SIDE - back, SIDE), block, pl.ds(first, half), :]
            lhs_ref[head * half : (head + 1) * half, n * BLK : (n + 1) * BLK] = rows
    rhs = jnp.concatenate([piece[...] for piece in pieces], axis=0)
    res = dot(lhs_ref[...], rhs).astype(jnp.bfloat16)
    own[...] = res[:half]
    for n in range(SIDE - 1):
        rest[n] = res[(n + 1) * half : (n + 2) * half]


def weight_part(side, place, mark, atts, pieces):
    width = pieces[0].shape[1]
    half = HD // 2
    return pl.pallas_call(
        functools.partial(weight_kernel, side),
        in_specs=[SMEM, ANY] + [VMEM] * (1 + len(pieces)),
        out_specs=[VMEM, VMEM],
        out_shape=[shaped(half, width), shaped(SIDE - 1, half, width)],
        scratch_shapes=[pltpu.VMEM((SIDE * half, SIDE * BLK), jnp.bfloat16)],
        compiler_params=SMALL,
        cost_estimate=cost(2 * 256 * 512 * 2048, 4 * MIB),
        name="weight_part",
    )(place, mark, atts, *pieces)


def assemble_kernel(scale, place_ref, kept, given, out_ref):
    half = kept.shape[0]
    for side, rows in enumerate((kept, given)):
        first = lax.rem(place_ref[1] + side, 2) * half
        out_ref[pl.ds(pl.multiple_of(first, half), half), :] = rows[...].astype(jnp.float32) * scale


def assemble(place, kept, given, scale):
    return pl.pallas_call(
        functools.partial(assemble_kernel, scale),
        in_specs=[SMEM, VMEM, VMEM],
        out_specs=VMEM,
        out_shape=shaped(HD, kept.shape[1], dtype=jnp.float32),
        compiler_params=SMALL,
        cost_estimate=cost(0, 2 * MIB),
        name="assemble",
    )(place, kept, given)


def after(a, other):
    return pl.pallas_call(
        lambda *refs: None,
        in_specs=[ANY, ANY],
        out_specs=ANY,
        out_shape=shaped(*a.shape),
        input_output_aliases={0: 0},
        compiler_params=SMALL,
        cost_estimate=cost(0, 0),
        name="after",
    )(a, other)


def shift_x(a, d):
    return lax.ppermute(a, "seq", [(s, s // SIDE * SIDE + (s + d) % SIDE) for s in range(SIDE**2)])


def shift_z(a, d):
    return lax.ppermute(a, "seq", [(s, (s + d * SIDE) % SIDE**2) for s in range(SIDE**2)])


def shift_y(a, d):
    return lax.ppermute(a, "dp", [(s, (s + 2 * d) % 8) for s in range(8)])


def sibling(a):
    return lax.ppermute(a, "dp", [(s, s ^ 1) for s in range(8)])


def wide(a):
    return a.astype(jnp.float32)


def on_device(saved_query, saved_key, saved_value, out_grad, out_weight, block_index, block_count):
    seq_at = lax.axis_index("seq")
    core = lax.axis_index("dp") % 2
    z, x = seq_at // SIDE, seq_at % SIDE
    ids, count = block_index[0], block_count[0]
    place = jnp.stack([z, core, x]).astype(jnp.int32)

    def by_seq(a):
        return lax.all_to_all(a, "seq", split_axis=0, concat_axis=0, tiled=True)

    packed = pack(saved_query[0], saved_key[0], saved_value[0], out_grad[0], out_weight)
    rows = by_seq(packed)
    pieces = [out_grad[0]] + [shift_x(out_grad[0], d) for d in HOPS[1:]]

    order = by_count(count)
    attention, norms = attention_forward(ids, count, order, rows)
    atts = lax.all_to_all(
        attention.reshape(SIDE, SIDE, HD, BLK),
        "seq",
        split_axis=0,
        concat_axis=0,
        axis_index_groups=[[i * SIDE + n for i in range(SIDE)] for n in range(SIDE)],
        tiled=True,
    )
    grads, mark = attention_backward(ids, count, order, rows, norms)

    give_own, give_rest = weight_part(1, place, mark, atts, pieces)
    given = sibling(give_rest)
    keep_own, keep_rest = weight_part(0, place, mark, atts, pieces)
    theirs = [(wide(keep_rest[n]) + wide(given[n])).astype(jnp.bfloat16) for n in range(SIDE - 1)]
    part = theirs[0].shape[0] // 2
    lead = shift_z(theirs[0][:part], -1)
    sent = [jnp.concatenate([lead, shift_z(theirs[0][part:], -1)], axis=0)]
    sent += [shift_z(rows, -d) for rows, d in zip(theirs[1:], HOPS[2:])]
    token_grads = unpack(by_seq(after(grads, lead[:16, :128])))
    row = wide(keep_own) + wide(sibling(give_own))
    for rows in sent:
        row = row + wide(rows)
    row = row.astype(jnp.bfloat16)
    ahead, behind, across = shift_y(row, 1), shift_y(row, -1), shift_y(row, 2)
    total = ((wide(row) + wide(across)) + (wide(ahead) + wide(behind))).astype(jnp.bfloat16)
    weight_scale = (BLK * SIDE**2 * 8) ** (-0.5)
    weight_grad = assemble(place, total, sibling(total), weight_scale)
    return *(grad[None] for grad in token_grads), weight_grad


def solution(mesh):
    placed = P("dp", "seq", None)
    return jax.shard_map(
        on_device,
        mesh=mesh,
        in_specs=(placed, placed, placed, placed, P(), P("dp", None, None), P("dp", None)),
        out_specs=(placed, placed, placed, P("seq", None)),
        check_vma=False,
    )
```
